32 devices in a mesh: seq: 16 (over z, x, core), fsdp: 2 (over y).
Axes of the slice: x: 2, y: 2, z: 4, core: 2. Of those that a mesh axis runs over, the one named last changes fastest.
Arguments:
- hidden_in: bfloat16 [2, 6144, 1792], P('fsdp', 'seq'), may hold values from -18 to 18
- cotangent: bfloat16 [2, 6144, 1792], P('fsdp', 'seq'), may hold values from -6 to 6
- mixer_weight: float32 [1792, 5888], P(('seq', 'fsdp')), may hold values from -0.88731955 to 0.88731955
- output_weight: float32 [1792, 1792], P(('seq', 'fsdp')), may hold values from -0.125 to 0.125
- updown_weight: float32 [1792, 8192], P(('seq', 'fsdp')), may hold values from -0.125 to 0.125
- down_weight: float32 [4096, 1792], P(('seq', 'fsdp')), may hold values from -0.09375 to 0.09375
- gain_weight: float32 [1792, 5], P(('seq', 'fsdp')), may hold values from -1.5 to 3.4
- mixer_first: float32 [1792, 5888], P(('seq', 'fsdp')), may hold values from -0.00010681152 to 0.00010681152
- output_first: float32 [1792, 1792], P(('seq', 'fsdp')), may hold values from -0.00010681152 to 0.00010681152
- updown_first: float32 [1792, 8192], P(('seq', 'fsdp')), may hold values from -0.00010681152 to 0.00010681152
- down_first: float32 [4096, 1792], P(('seq', 'fsdp')), may hold values from -0.00010681152 to 0.00010681152
- gain_first: float32 [1792, 5], P(('seq', 'fsdp')), may hold values from -0.0004272461 to 0.0004272461
- mixer_second: float32 [1792, 5888], P(('seq', 'fsdp')), may hold values from 1.4807937e-09 to 5.867296e-09
- output_second: float32 [1792, 1792], P(('seq', 'fsdp')), may hold values from 1.4807937e-09 to 5.867296e-09
- updown_second: float32 [1792, 8192], P(('seq', 'fsdp')), may hold values from 1.4807937e-09 to 5.867296e-09
- down_second: float32 [4096, 1792], P(('seq', 'fsdp')), may hold values from 1.4807937e-09 to 5.867296e-09
- gain_second: float32 [1792, 5], P(('seq', 'fsdp')), may hold values from 3.9115307e-09 to 1.5646123e-08
- lengths: int32 [2, 8], P('fsdp'), may hold values from 1 to 3072, 6144 in all within a row
- seq_order: int32 [2, 8], P('fsdp'), may hold values from 0 to 7, each once within a row
- pad_mask: int32 [2, 6144], P('fsdp'), may hold values 0 or 1
Outputs:
- layer_output: bfloat16 [2, 6144, 1792], P('fsdp', 'seq')
- input_grad: float32 [2, 6144, 1792], P('fsdp', 'seq')
- mixer_next: float32 [1792, 5888], P(('seq', 'fsdp'))
- output_next: float32 [1792, 1792], P(('seq', 'fsdp'))
- updown_next: float32 [1792, 8192], P(('seq', 'fsdp'))
- down_next: float32 [4096, 1792], P(('seq', 'fsdp'))
- gain_next: float32 [1792, 5], P(('seq', 'fsdp'))
- mixer_momentum: float32 [1792, 5888], P(('seq', 'fsdp'))
- output_momentum: float32 [1792, 1792], P(('seq', 'fsdp'))
- updown_momentum: float32 [1792, 8192], P(('seq', 'fsdp'))
- down_momentum: float32 [4096, 1792], P(('seq', 'fsdp'))
- gain_momentum: float32 [1792, 5], P(('seq', 'fsdp'))
- mixer_variance: float32 [1792, 5888], P(('seq', 'fsdp'))
- output_variance: float32 [1792, 1792], P(('seq', 'fsdp'))
- updown_variance: float32 [1792, 8192], P(('seq', 'fsdp'))
- down_variance: float32 [4096, 1792], P(('seq', 'fsdp'))
- gain_variance: float32 [1792, 5], P(('seq', 'fsdp'))
- grad_norm: float32 [], replicated
- layer_rms: float32 [3], replicated
The draws below stay inside these ranges and needn't reach their ends.
Inputs may be any that keep to these rules, and one draw needn't show every extreme that they name: Each pack's 8 lengths sum to 6144, the largest is exactly 3072. Each row is a permutation; sequence seq_order[p] stands p-th in its pack.
All inputs are finite; a program needn't handle non-finite values. No bound on the sum of `pad_mask` on one device may be relied on, other than what follows from the above.
Results may differ from the reference program's by a relative error of at most 0.015.
The reference program's roundings to bfloat16 on the way count: a program that leaves them out, or rounds other values in their place, can miss the bound.
Values may be sent and summed in bfloat16 or wider, within the bound.
A program may use at most 384 MiB of HBM per device.

```python
import math
import jax
import jax.numpy as jnp
import numpy as np
from jax import lax

D = 1792
HEADS = 16
FEAT = 16
FF = 4096
SEQS = 8
BLOCK = 512
STEP = 10
QK = 256
IN_COLS = 5888
ROWS = 6144
MAXLEN = 3072
PARAMS = 35791616
N_FSDP = 2


def draw_hidden_in(key, part):
    key = jax.random.fold_in(key, 11)
    shape = (N_FSDP, ROWS, D)
    group = jnp.arange(N_FSDP, dtype=jnp.float32)[:, None, None] / max(N_FSDP - 1, 1)
    place = jnp.arange(ROWS, dtype=jnp.float32)[None, :, None] / ROWS
    base = jnp.clip(jax.random.normal(key, shape, jnp.float32), -6.0, 6.0)
    rise = 0.73
    return (base * (1.0 + rise * group) * (1.0 + rise * place)).astype(jnp.bfloat16)


def draw_gain_weight(key, part):
    key = jax.random.fold_in(key, 12)
    gain_key, tap_key = jax.random.split(key)
    rising = 1.0 + 2.0 * jnp.arange(D, dtype=jnp.float32)[:, None] / D
    gains = rising * (1.0 + 0.1 * jax.random.uniform(gain_key, (D, 2), jnp.float32, -1.0, 1.0))
    taps = 0.5 * jnp.clip(jax.random.normal(tap_key, (D, 3), jnp.float32), -3.0, 3.0)
    return jnp.concatenate([gains, taps], axis=1)


def draw_mixer_weight(key, part):
    key = jax.random.fold_in(key, 13)
    base = jnp.clip(jax.random.normal(key, (D, IN_COLS), jnp.float32), -6.0, 6.0) / D ** 0.5
    columns = jnp.arange(IN_COLS, dtype=jnp.int32)
    scale = jnp.where((columns >= 2 * QK) & (columns < 2 * QK + D), float((MAXLEN // 2) ** 0.25), 1.0)
    return base * scale[None, :]


def set_ends(entries, rng, low, largest):
    shape = entries.shape
    spot = [jax.random.randint(jax.random.fold_in(rng, axis), (), 0, shape[axis]) for axis in range(len(shape))]
    entries = entries.at[tuple(spot)].set(low)
    longest = shape.index(max(shape))
    spot[longest] = (spot[longest] + 1) % shape[longest]
    return entries.at[tuple(spot)].set(largest)


def block_levels(key, shape, cuts, low, top_value):
    level, own = 1.0, jax.random.fold_in(key, 6)
    for axis_at, blocks in cuts:
        draws = jnp.exp(jax.random.uniform(jax.random.fold_in(own, axis_at), (blocks,), jnp.float32, low / len(cuts), top_value / len(cuts)))
        level = level * jnp.repeat(draws, shape[axis_at] // blocks).reshape([-1 if axis == axis_at else 1 for axis in range(len(shape))])
    return level


def profile(number_of, total, reach, lean):
    weights = [(1 << 20) // math.isqrt(grade ** lean) + 1 for grade in range(2, number_of + 1)]
    rest, counts = total - reach - (number_of - 1), [1] * (number_of - 1)
    while rest > 0:
        movable = [i for i in range(number_of - 1) if counts[i] < reach]
        pool, remaining = sum([weights[i] for i in movable]), rest
        for i in movable:
            extra = min(reach - counts[i], max(1, remaining * weights[i] // pool), rest)
            counts[i] = counts[i] + extra
            rest = rest - extra
    return np.array([reach] + counts)


def uneven_parts(rng, number_of, total, most, slope):
    if number_of == 2:
        one = jax.random.randint(rng, (), max(1, total - most), min(most, total - 1) + 1)
        return jnp.stack([one, total - one])
    sizes = jnp.asarray(profile(number_of, total, most, slope), jnp.int32)
    pairs = (number_of - 1) // 2
    source_of, receiver = sizes[1:1 + 2 * pairs:2], sizes[2:2 + 2 * pairs:2]
    room = jnp.minimum(source_of - 1, most - receiver)
    passed = jax.random.randint(jax.random.fold_in(rng, 1), (pairs,), 0, 1 << 20) % (room + 1)
    sizes = sizes.at[1:1 + 2 * pairs:2].set(source_of - passed).at[2:2 + 2 * pairs:2].set(receiver + passed)
    return sizes[jax.random.permutation(jax.random.fold_in(rng, 2), number_of)]


def bell_draw(own_key, dims, deviation, most, shards=(), kind=jnp.bfloat16):
    values = jax.random.normal(own_key, dims, jnp.float32) * deviation
    if len(shards) > 0:
        values = block_levels(own_key, dims, shards, -0.22, 0.18) * values
    return jnp.clip(values, min=-most, max=most).astype(kind)


def setup_inputs(seed: int = 0) -> dict:
    seeds = jax.random.split(jax.random.key(seed), 21)
    return {
        "hidden_in": draw_hidden_in(jax.random.fold_in(seeds[20], 71), 0),
        "cotangent": bell_draw(seeds[1], (N_FSDP, ROWS, D), 1.0, 6.0, ((0, 2), (1, 16))),
        "mixer_weight": draw_mixer_weight(jax.random.fold_in(seeds[20], 71), 0),
        "output_weight": bell_draw(seeds[3], (D, D), D ** -0.5, 0.125, ((0, 32),), jnp.float32),
        "updown_weight": bell_draw(seeds[4], (D, 2 * FF), D ** -0.5, 0.125, ((0, 32),), jnp.float32),
        "down_weight": bell_draw(seeds[5], (FF, D), FF ** -0.5, 0.09375, ((0, 32),), jnp.float32),
        "gain_weight": draw_gain_weight(jax.random.fold_in(seeds[20], 71), 0),
        "mixer_first": bell_draw(seeds[7], (D, IN_COLS), (0.11 / PARAMS ** 0.5), 0.00010681152, ((0, 32),), jnp.float32),
        "output_first": bell_draw(seeds[8], (D, D), (0.11 / PARAMS ** 0.5), 0.00010681152, ((0, 32),), jnp.float32),
        "updown_first": bell_draw(seeds[9], (D, 2 * FF), (0.11 / PARAMS ** 0.5), 0.00010681152, ((0, 32),), jnp.float32),
        "down_first": bell_draw(seeds[10], (FF, D), (0.11 / PARAMS ** 0.5), 0.00010681152, ((0, 32),), jnp.float32),
        "gain_first": bell_draw(seeds[11], (D, 5), (0.44 / PARAMS ** 0.5), 0.0004272461, ((0, 32),), jnp.float32),
        "mixer_second": jnp.clip(jnp.exp(math.log(5.867295982397991e-09) - 1.37681564 * jax.random.uniform(seeds[12], (D, IN_COLS), jnp.float32) ** block_levels(seeds[12], (D, IN_COLS), ((0, 32),), -0.2, 0.2)), 1.4807937098737511e-09, 5.867295982397991e-09),
        "output_second": jnp.clip(jnp.exp(math.log(5.867295982397991e-09) - 1.37681564 * jax.random.uniform(seeds[13], (D, D), jnp.float32) ** block_levels(seeds[13], (D, D), ((0, 32),), -0.2, 0.2)), 1.4807937098737511e-09, 5.867295982397991e-09),
        "updown_second": jnp.clip(jnp.exp(math.log(5.867295982397991e-09) - 1.37681564 * jax.random.uniform(seeds[14], (D, 2 * FF), jnp.float32) ** block_levels(seeds[14], (D, 2 * FF), ((0, 32),), -0.2, 0.2)), 1.4807937098737511e-09, 5.867295982397991e-09),
        "down_second": jnp.clip(jnp.exp(math.log(5.867295982397991e-09) - 1.37681564 * jax.random.uniform(seeds[15], (FF, D), jnp.float32) ** block_levels(seeds[15], (FF, D), ((0, 32),), -0.2, 0.2)), 1.4807937098737511e-09, 5.867295982397991e-09),
        "gain_second": jnp.clip(jnp.exp(math.log(1.5646122619727976e-08) - 1.3862944 * jax.random.uniform(seeds[16], (D, 5), jnp.float32) ** block_levels(seeds[16], (D, 5), ((0, 32),), -0.2, 0.2)), 3.911530654931994e-09, 1.5646122619727976e-08),
        "lengths": jax.vmap(lambda own: uneven_parts(own, SEQS, ROWS, MAXLEN, 2))(jax.random.split(seeds[17], N_FSDP)).reshape((N_FSDP, SEQS)).astype(jnp.int32),
        "seq_order": jax.vmap(lambda own: jax.random.permutation(own, SEQS))(jax.random.split(seeds[18], N_FSDP)).reshape((N_FSDP, SEQS)).astype(jnp.int32),
        "pad_mask": set_ends((jax.random.randint(seeds[19], (N_FSDP, ROWS), 0, 8) < 7).astype(jnp.int32), jax.random.fold_in(seeds[19], 1), 0, 1),
    }


highest = lax.Precision.HIGHEST
norm_eps = 1e-06
beta_one = 0.9
beta_two = 0.95
adam_eps = 1e-08
rate_matrix = 0.05
rate_gain = 1.5
decay_rate = 0.1
clip_level = 1.0

@jax.custom_vjp
def low(v):
    return lax.optimization_barrier(v.astype(jnp.bfloat16)).astype(jnp.float32)

@jax.custom_vjp
def low_back(v):
    return v

def low_keep(v):
    return (low(v), None)

def low_pass(kept, grad):
    return (grad,)

def back_keep(v):
    return (v, None)

def back_low(kept, grad):
    return (low(grad),)
low.defvjp(low_keep, low_pass)
low_back.defvjp(back_keep, back_low)

def taylor(vectors):
    feature_count = vectors.shape[-1]
    quad = (vectors[..., :, None] * vectors[..., None, :]).reshape(vectors.shape[:-1] + (feature_count * feature_count,))
    ones_col = jnp.ones(vectors.shape[:-1] + (1,), vectors.dtype)
    return jnp.concatenate([ones_col, vectors * feature_count ** (-0.25), quad * (2.0 * feature_count) ** (-0.5)], axis=-1)

def block_step(carried, block_in):
    state, totals, last_seg = carried
    query, key_vecs, value, keep, segment = block_in
    feature_count = query.shape[-1]
    length = query.shape[0]
    dots = jnp.einsum('ihf,jhf->hij', query, key_vecs, precision=highest) * feature_count ** (-0.5)
    kernel = 1.0 + dots + 0.5 * dots * dots
    row_ids = lax.broadcasted_iota(jnp.int32, (length, length), 0)
    col_ids = lax.broadcasted_iota(jnp.int32, (length, length), 1)
    allowed = jnp.where((segment[:, None] == segment[None, :]) & (col_ids <= row_ids), keep[None, :], 0.0)
    scores = kernel * allowed[None, :, :]
    numer = jnp.einsum('hij,jhv->ihv', scores, value, precision=highest)
    denom = lax.optimization_barrier(jnp.sum(scores, axis=2)).T
    carried_on = (segment == last_seg).astype(query.dtype)
    query_map = taylor(query)
    numer = numer + carried_on[:, None, None] * jnp.einsum('iht,htv->ihv', query_map, state, precision=highest)
    denom = denom + carried_on[:, None] * jnp.einsum('iht,ht->ih', query_map, totals, precision=highest)
    output = numer / (denom[:, :, None] + 1.0)
    tail_seg = segment[length - 1].astype(jnp.int32)
    holding = (tail_seg == last_seg).astype(query.dtype)
    fresh = jnp.where(segment == tail_seg, keep, 0.0)
    key_map = taylor(key_vecs) * fresh[:, None, None]
    state = holding * state + jnp.einsum('jht,jhv->htv', key_map, value, precision=highest)
    totals = holding * totals + lax.optimization_barrier(jnp.sum(key_map, axis=0))
    return ((state, totals, tail_seg), output)

def attention(query, key_vecs, value, keep, segment, block_rows):
    total = query.shape[0]
    heads = query.shape[1]
    feature_count = query.shape[2]
    width = value.shape[2]
    blocks = total // block_rows
    features = 1 + feature_count + feature_count * feature_count

    def split_rows(array):
        return array.reshape((blocks, block_rows) + array.shape[1:])
    start = (jnp.zeros((heads, features, width), query.dtype), jnp.zeros((heads, features), query.dtype), jnp.array(-1, jnp.int32))
    inputs = (split_rows(query), split_rows(key_vecs), split_rows(value), split_rows(keep), split_rows(segment.astype(jnp.int32)))
    ignored, outputs = lax.scan(jax.checkpoint(block_step), start, inputs)
    return outputs.reshape(total, heads, width)

def short_conv(extended, taps, seg_ext, count):
    result = jnp.zeros((count, extended.shape[1]), extended.dtype)
    for shift_by in range(3):
        piece = lax.slice_in_dim(extended, 2 - shift_by, 2 - shift_by + count, axis=0)
        earlier = lax.slice_in_dim(seg_ext, 2 - shift_by, 2 - shift_by + count, axis=0)
        same = (earlier == seg_ext[2:]).astype(extended.dtype)
        result = result + taps[shift_by][None, :] * piece * same[:, None]
    return result

def norm_scale(values, gain):
    return values * lax.rsqrt(lax.optimization_barrier(jnp.mean(values * values, axis=-1, keepdims=True)) + norm_eps) * gain

def segment_of(lengths_row, order_row, positions):
    count = lengths_row.shape[0]
    picks = order_row[:, None] == jnp.arange(count, dtype=jnp.int32)[None, :]
    ordered = lax.optimization_barrier(jnp.sum(jnp.where(picks, lengths_row[None, :], 0), axis=1)).astype(jnp.int32)
    ends = jnp.cumsum(ordered).astype(jnp.int32)
    return lax.optimization_barrier(jnp.sum((positions[:, None] >= ends[None, :]).astype(jnp.int32), axis=1)).astype(jnp.int32)

def adam_step(weight, first, second, grad, rate, decay):
    momentum = beta_one * first + (1.0 - beta_one) * grad
    variance = beta_two * second + (1.0 - beta_two) * grad * grad
    corrected = momentum / (1.0 - beta_one ** STEP)
    scaled = variance / (1.0 - beta_two ** STEP)
    return (weight - rate * (corrected / (jnp.sqrt(scaled) + adam_eps) + decay * weight), momentum, variance)

def group_forward(tokens_in, mixer, outer, updown, down, gains, segment, keep):
    count = tokens_in.shape[0]
    qk_cols = HEADS * FEAT
    normed = low(norm_scale(tokens_in, gains[:, 0]))
    proj = low_back(jnp.dot(normed, mixer, precision=highest))
    query = low(proj[:, :qk_cols])
    key_vecs = low(proj[:, qk_cols:2 * qk_cols])
    value = low(proj[:, 2 * qk_cols:2 * qk_cols + D])
    conv_in = low(proj[:, 2 * qk_cols + D:2 * qk_cols + 2 * D])
    gate = proj[:, 2 * qk_cols + 2 * D:]
    att = attention(query.reshape(count, HEADS, FEAT), key_vecs.reshape(count, HEADS, FEAT), value.reshape(count, HEADS, D // HEADS), keep, segment, BLOCK).reshape(count, D)
    extended = jnp.concatenate([jnp.zeros((2, D), tokens_in.dtype), conv_in], axis=0)
    seg_ext = jnp.concatenate([jnp.full((2,), -1, jnp.int32), segment.astype(jnp.int32)])
    gated = short_conv(extended, gains[:, 2:5].T, seg_ext, count) * jax.nn.sigmoid(gate)
    mix = low(low_back(low(att) + gated))
    branch = low_back(jnp.dot(mix, outer, precision=highest))
    middle = tokens_in + branch
    normed2 = low(norm_scale(middle, gains[:, 1]))
    gateup = low_back(jnp.dot(normed2, updown, precision=highest))
    inner = low(low_back(jax.nn.silu(gateup[:, :FF]) * gateup[:, FF:]))
    feed = low_back(jnp.dot(inner, down, precision=highest))
    sums = jnp.stack([jnp.sum(middle * middle), jnp.sum(branch * branch), jnp.sum(feed * feed)])
    return (middle + feed, sums)

def reference(hidden_in, cotangent, mixer_weight, output_weight, updown_weight, down_weight, gain_weight, mixer_first, output_first, updown_first, down_first, gain_first, mixer_second, output_second, updown_second, down_second, gain_second, lengths, seq_order, pad_mask):
    masters = (mixer_weight, output_weight, updown_weight, down_weight, gain_weight)
    firsts = (mixer_first, output_first, updown_first, down_first, gain_first)
    seconds = (mixer_second, output_second, updown_second, down_second, gain_second)
    weights_low = [w.astype(jnp.bfloat16).astype(jnp.float32) for w in masters]
    positions = jnp.arange(ROWS, dtype=jnp.int32)
    segments = jax.vmap(lambda lens_row, order_row: segment_of(lens_row, order_row, positions))(lengths, seq_order).astype(jnp.int32)
    keep_all = pad_mask.astype(jnp.float32)

    def forward(tokens_all, mixer, outer, updown, down, gains):
        outputs, sums = jax.vmap(lambda tok_group, seg_group, keep_group: group_forward(tok_group, mixer, outer, updown, down, gains, seg_group, keep_group))(tokens_all, segments, keep_all)
        return (outputs, lax.optimization_barrier(jnp.sum(sums, axis=0)))
    layer, back_fn, sums = jax.vjp(forward, hidden_in.astype(jnp.float32), *weights_low, has_aux=True)
    grads = back_fn(cotangent.astype(jnp.float32))
    input_grad = grads[0]
    weight_grads = grads[1:]
    total_sq = jnp.float32(0.0)
    for grad_one in weight_grads:
        total_sq = total_sq + jnp.sum(grad_one * grad_one)
    grad_norm = jnp.sqrt(total_sq)
    factor = jnp.minimum(1.0, clip_level / grad_norm)
    nexts, moms, varis = ([], [], [])
    for index in range(5):
        rate = rate_gain if index == 4 else rate_matrix
        decay = 0.0 if index == 4 else decay_rate
        new_w, new_m, new_v = adam_step(masters[index], firsts[index], seconds[index], weight_grads[index] * factor, rate, decay)
        nexts.append(new_w)
        moms.append(new_m)
        varis.append(new_v)
    layer_rms = jnp.sqrt(sums / (N_FSDP * ROWS * D))
    return (layer.astype(jnp.bfloat16), input_grad, nexts[0], nexts[1], nexts[2], nexts[3], nexts[4], moms[0], moms[1], moms[2], moms[3], moms[4], varis[0], varis[1], varis[2], varis[3], varis[4], grad_norm, layer_rms)
```

```python
import functools

import jax
import jax.numpy as jnp
import numpy as np
from jax import lax
from jax.experimental import pallas as pl
from jax.experimental.layout import Layout, with_layout_constraint
from jax.experimental.pallas import tpu as pltpu
from jax.sharding import Mesh
from jax.sharding import PartitionSpec as P

D = 1792
HEADS = 16
FEAT = 16
FF = 4096
STEP = 10
HALF_HEADS = HEADS // 2
HEAD_WIDTH = D // HEADS
PHI = 160
LANES = 128
TILE = 256

norm_eps = 1e-06
beta_one = 0.9
beta_two = 0.95
adam_eps = 1e-08
rate_matrix = 0.05
rate_gain = 1.5
decay_rate = 0.1
clip_level = 1.0

bf16 = jnp.bfloat16
f32 = jnp.float32
VMEM_LIMIT = 48 * 1024 * 1024
GATHER_PACE = (-2.0, -1.2, 0.0, 1.1)
REDUCE_PACE = (0.0, 1.5, 2.6, 3.7, 4.8)


def feature_tables():
    first = np.zeros((FEAT, PHI), np.float32)
    second = np.zeros((FEAT, PHI), np.float32)
    bias = np.zeros((2, PHI), np.float32)
    scale = np.zeros((PHI,), np.float32)
    bias[:, 0] = 1.0
    scale[0] = 1.0
    at = 1
    for a in range(FEAT):
        first[a, at] = 1.0
        bias[1, at] = 1.0
        scale[at] = FEAT**-0.5
        at += 1
    for a in range(FEAT):
        for b in range(a, FEAT):
            first[a, at] = 1.0
            second[b, at] = 1.0
            scale[at] = (1.0 if a == b else 2.0) / (2.0 * FEAT)
            at += 1
    return first, second, bias, scale


def dot_nn(a, b):
    return lax.dot_general(a, b, (((1,), (0,)), ((), ())), preferred_element_type=f32)


def dot_tn(a, b):
    return lax.dot_general(a, b, (((0,), (0,)), ((), ())), preferred_element_type=f32)


def dot_nt(a, b):
    return lax.dot_general(a, b, (((1,), (1,)), ((), ())), preferred_element_type=f32)


def bits_of(size):
    return size.bit_length() - 1


def other(axis, bit):
    me = lax.axis_index(axis)
    return {axis: me + (1 - 2 * ((me // 2**bit) % 2)) * 2**bit}


def greet(partners):
    barrier = pltpu.get_barrier_semaphore()
    for partner in partners:
        pl.semaphore_signal(barrier, inc=1, device_id=partner, device_id_type=pl.DeviceIdType.MESH)
    pl.semaphore_wait(barrier, len(partners))


def gather_kernel(ring, groups, parts, orders, count, shared, *refs):
    in_refs, out_refs = refs[:count], refs[count : 2 * count]
    send_sem, recv_sem, own_sem = refs[2 * count :]
    ring_bits, group_bits = bits_of(ring), bits_of(groups)
    every = [("ring", b) for b in reversed(range(ring_bits))] + [("fsdp", b) for b in reversed(range(group_bits))]
    partners = {key: other(*key) for key in every}
    core_partner = other("core", 0)
    greet(list(partners.values()) + [core_partner])
    core = lax.axis_index("core")
    bit = {(axis, b): (lax.axis_index(axis) // 2**b) % 2 for axis, b in every}

    def view(ref, have, columns):
        spots = [slice(None) if key in have else pl.ds(bit[key], 1) for key in every]
        spots.insert(ring_bits, slice(None))
        return ref.at[tuple(spots) + (slice(None), columns)]

    def placed(part):
        index, at, width = parts[part]
        if index not in shared:
            return pl.ds(at, width)
        return pl.ds(pl.multiple_of(core * in_refs[index].shape[-1] + at, LANES), width)

    steps = len(every)
    events = []
    for part in range(len(parts)):
        for step in range(steps):
            late = GATHER_PACE[min(max(step + 4 - steps, 0), 3)]
            events.append((part // 2 + late, part, step))
    copies, owns = {}, []
    for index in range(count):
        everything = slice(None)
        if index in shared:
            columns = in_refs[index].shape[-1]
            everything = pl.ds(pl.multiple_of(core * columns, LANES), columns)
        owns.append(
            pltpu.make_async_copy(in_refs[index], view(out_refs[index], (), everything), own_sem.at[index])
        )
    owned = False
    for _, part, step in sorted(events):
        if step and not owned:
            owned = True
            for own in owns:
                own.start()
            for own in owns:
                own.wait()
        order = orders[part % len(orders)]
        if step:
            copies[part, step - 1].wait_recv()
        index, at, width = parts[part]
        ndim = in_refs[index].ndim
        here = view(out_refs[index], order[:step], placed(part))
        source = in_refs[index].at[(slice(None),) * (ndim - 1) + (pl.ds(at, width),)] if step == 0 else here
        copies[part, step] = pltpu.make_async_remote_copy(
            src_ref=source,
            dst_ref=here,
            send_sem=send_sem.at[part, step],
            recv_sem=recv_sem.at[part, step],
            device_id=partners[order[step]],
            device_id_type=pl.DeviceIdType.MESH,
        )
        copies[part, step].start()
    for part in range(len(parts)):
        copies[part, steps - 1].wait_recv()
        if parts[part][0] in shared:
            here = view(out_refs[parts[part][0]], every, placed(part))
            copies[part, steps] = pltpu.make_async_remote_copy(
                src_ref=here,
                dst_ref=here,
                send_sem=send_sem.at[part, steps],
                recv_sem=recv_sem.at[part, steps],
                device_id=core_partner,
                device_id_type=pl.DeviceIdType.MESH,
            )
            copies[part, steps].start()
    for part in range(len(parts)):
        if parts[part][0] in shared:
            copies[part, steps].wait_recv()
    for copy in copies.values():
        copy.wait_send()


def gather_rows(blocks, cuts, shared, ring, groups):
    ring_bits, group_bits = bits_of(ring), bits_of(groups)
    near, far = [("ring", 0)], [("ring", b) for b in reversed(range(1, ring_bits))]
    group = [("fsdp", b) for b in reversed(range(group_bits))]
    orders = (far + near + group, far + group + near)
    parts = []
    for index, widths in enumerate(cuts):
        at = 0
        for width in widths:
            parts.append((index, at, width))
            at += width
    steps = ring_bits + group_bits
    ins, shapes, size = [], [], 0
    for block in blocks:
        cores, rows, columns = block.shape
        ins.append(block.reshape((1,) * ring_bits + (cores,) + (1,) * group_bits + (rows, columns)))
        width = 2 * columns if len(ins) - 1 in shared else columns
        shape = (2,) * ring_bits + (cores,) + (2,) * group_bits + (rows, width)
        shapes.append(jax.ShapeDtypeStruct(shape, block.dtype))
        size += 2 * block.size * ring * groups
    outs = pl.pallas_call(
        functools.partial(gather_kernel, ring, groups, parts, orders, len(blocks), shared),
        in_specs=[pl.BlockSpec(memory_space=pl.ANY)] * len(blocks),
        out_specs=[pl.BlockSpec(memory_space=pl.ANY)] * len(blocks),
        out_shape=shapes,
        scratch_shapes=[
            pltpu.SemaphoreType.DMA((len(parts), steps + 1)),
            pltpu.SemaphoreType.DMA((len(parts), steps + 1)),
            pltpu.SemaphoreType.DMA((len(blocks),)),
        ],
        compiler_params=pltpu.CompilerParams(collective_id=0, has_side_effects=True),
        cost_estimate=pl.CostEstimate(flops=0, bytes_accessed=20 * size, transcendentals=0),
        name="gather_rows",
    )(*ins)
    return [o.reshape((2 * ring * groups if b.shape[0] == 2 else ring * groups) * b.shape[1], o.shape[-1])
            for o, b in zip(outs, blocks)]


def reduce_kernel(chains, partners, pairs, *refs):
    refs = list(refs)

    def take(number):
        taken = refs[:number]
        del refs[:number]
        return taken

    in_refs, out_refs = take(pairs), take(len(chains))
    own_refs = take(len(chains))
    recv_refs = [take(len(chain[4])) for chain in chains]
    send_refs = [take(len(chain[4]) - 1) for chain in chains]
    send_sem, recv_sem, own_sem = take(3)
    greet([other(*key) for key in partners])
    mine = {(axis, b): (lax.axis_index(axis) // 2**b) % 2 for axis, b in partners}
    copies = {}

    def start(c, step, source):
        copies[c, step] = pltpu.make_async_remote_copy(
            src_ref=source,
            dst_ref=recv_refs[c][step],
            send_sem=send_sem.at[c, step],
            recv_sem=recv_sem.at[c, step],
            device_id=other(*chains[c][4][step]),
            device_id_type=pl.DeviceIdType.MESH,
        )
        copies[c, step].start()

    def first_half(c, side):
        source, at, width, keys, order, rank = chains[c]
        spots = tuple(side if key == order[0] else slice(None) for key in keys)
        return in_refs[source].at[spots + (slice(None), pl.ds(at, width))]

    def add_up(c, step, target):
        keys, order = chains[c][3], chains[c][4]
        left = [key for key in keys if key not in order[: step + 1]]
        rows = target.shape[-2]
        tile = 16 if rows % 16 == 0 else rows
        for spot in np.ndindex(*(2,) * len(left)):
            spot = tuple(int(i) for i in spot)
            free = dict(zip(left, spot))

            def where(key):
                if key in free:
                    return free[key]
                return 1 - mine[key] if step < len(order) and key == order[step] else mine[key]

            def body(i, carry):
                at = pl.ds(pl.multiple_of(i * tile, tile), tile)
                total = None
                for t in range(step + 1):
                    ref = own_refs[c] if t == 0 else recv_refs[c][t - 1]
                    index = tuple(where(key) for key in keys if key not in order[: max(t, 1)])
                    term = ref[index + (at, slice(None))].astype(f32)
                    total = term if total is None else total + term
                target[spot + (at, slice(None))] = total.astype(target.dtype)
                return carry

            lax.fori_loop(0, rows // tile, body, 0)

    owns = []
    for c in range(len(chains)):
        own = pltpu.make_async_copy(first_half(c, mine[chains[c][4][0]]), own_refs[c], own_sem.at[c])
        own.start()
        owns.append(own)
    events = []
    for c, chain in enumerate(chains):
        for step in range(len(chain[4]) + 1):
            events.append((chain[5] + REDUCE_PACE[min(step, 4)], c, step))
    for _, c, step in sorted(events):
        order = chains[c][4]
        if step == 0:
            start(c, 0, first_half(c, 1 - mine[order[0]]))
            continue
        if step == 1:
            owns[c].wait()
        copies[c, step - 1].wait_recv()
        if step < len(order):
            add_up(c, step, send_refs[c][step - 1])
            start(c, step, send_refs[c][step - 1])
        else:
            add_up(c, step, out_refs[c])
    for copy in copies.values():
        copy.wait_send()


def reduce_rest(arrays, specs):
    outs, owns, recvs, sends = [], [], [], []
    steps = 0
    for source, at, width, keys, order, rank in specs:
        rows = arrays[source].shape[-2]
        steps = max(steps, len(order))
        outs.append(jax.ShapeDtypeStruct((rows, width), f32))
        shapes = [(2,) * (len(keys) - step - 1) + (rows, width) for step in range(len(order))]
        owns.append(pltpu.VMEM(shapes[0], bf16))
        recvs += [pltpu.VMEM(shape, bf16) for shape in shapes]
        sends += [pltpu.VMEM(shape, bf16) for shape in shapes[1:]]
    partners = sorted({key for spec in specs for key in spec[4]})
    sems = (len(specs), steps)
    return pl.pallas_call(
        functools.partial(reduce_kernel, specs, partners, len(arrays)),
        in_specs=[pl.BlockSpec(memory_space=pl.ANY)] * len(arrays),
        out_specs=[pl.BlockSpec(memory_space=pltpu.VMEM)] * len(specs),
        out_shape=outs,
        scratch_shapes=owns
        + recvs
        + sends
        + [
            pltpu.SemaphoreType.DMA(sems),
            pltpu.SemaphoreType.DMA(sems),
            pltpu.SemaphoreType.DMA((len(specs),)),
        ],
        compiler_params=pltpu.CompilerParams(
            collective_id=2, has_side_effects=True, vmem_limit_bytes=58 * 1024 * 1024
        ),
        name="reduce_rest",
    )(*arrays)


def sum_kernel(partners, in_ref, out_ref, held, got, send_sem, recv_sem):
    partners = [other(*key) for key in partners]
    greet(partners)
    held[0] = in_ref[...]
    for step, partner in enumerate(partners):
        copy = pltpu.make_async_remote_copy(
            src_ref=held.at[step],
            dst_ref=got.at[step],
            send_sem=send_sem.at[step],
            recv_sem=recv_sem.at[step],
            device_id=partner,
            device_id_type=pl.DeviceIdType.MESH,
        )
        copy.start()
        copy.wait()
        total = held[step] + got[step]
        if step + 1 < len(partners):
            held[step + 1] = total
        else:
            out_ref[...] = total


def sum_everywhere(block, ring, groups):
    partners = [("core", 0)] + [("ring", b) for b in range(bits_of(ring))] + [("fsdp", b) for b in range(bits_of(groups))]
    steps = len(partners)
    return pl.pallas_call(
        functools.partial(sum_kernel, partners),
        in_specs=[pl.BlockSpec(memory_space=pltpu.VMEM)],
        out_specs=pl.BlockSpec(memory_space=pltpu.VMEM),
        out_shape=jax.ShapeDtypeStruct(block.shape, f32),
        scratch_shapes=[
            pltpu.VMEM((steps,) + block.shape, f32),
            pltpu.VMEM((steps,) + block.shape, f32),
            pltpu.SemaphoreType.DMA((steps,)),
            pltpu.SemaphoreType.DMA((steps,)),
        ],
        compiler_params=pltpu.CompilerParams(collective_id=1, has_side_effects=True),
        name="sum_everywhere",
    )(block)


def exchange(source, target, send_sem, recv_sem):
    ring = source.shape[0]
    me = lax.axis_index("ring")
    copies = []
    for away in range(1, ring):
        peer = (me + away) % ring
        copy = pltpu.make_async_remote_copy(
            src_ref=source.at[peer],
            dst_ref=target.at[me],
            send_sem=send_sem.at[away],
            recv_sem=recv_sem.at[away],
            device_id={"ring": peer},
            device_id_type=pl.DeviceIdType.MESH,
        )
        copy.start()
        copies.append(copy)
    target[me] = source[me]
    return copies


def pass_along(source, target, away, send_sem, recv_sem):
    ring = lax.axis_size("ring")
    copy = pltpu.make_async_remote_copy(
        src_ref=source,
        dst_ref=target,
        send_sem=send_sem,
        recv_sem=recv_sem,
        device_id={"ring": (lax.axis_index("ring") + ring + away) % ring},
        device_id_type=pl.DeviceIdType.MESH,
    )
    copy.start()
    return copy


def arrive(copies):
    for copy in copies:
        copy.wait_recv()


def leave(copies):
    for copy in copies:
        copy.wait_send()


def greet_ring(ring):
    me = lax.axis_index("ring")
    greet([{"ring": (me + away) % ring} for away in range(1, ring)])


def put_state(buffer, head, state):
    ring, piece = buffer.shape[0], buffer.shape[1]
    share = ring // HALF_HEADS
    for part in range(share):
        buffer[head * share + part] = state[part * piece : (part + 1) * piece].astype(bf16)


def get_state(buffer, head):
    share = buffer.shape[0] // HALF_HEADS
    if share == 1:
        return buffer[head]
    return jnp.concatenate([buffer[head * share + part] for part in range(share)], axis=0)


def linked(states, link_ref, target, backward):
    ring = states.shape[0]
    for d in range(ring):
        total = jnp.zeros(states.shape[1:], f32)
        for e in range(d + 1, ring) if backward else range(d):
            weight = link_ref[e, d] if backward else link_ref[d, e]
            total = total + weight * states[e].astype(f32)
        target[d] = total.astype(bf16)


def attend_kernel(
    ring, link_ref, q_ref, kt_ref, v_ref, allow_ref, on_ref, fresh_ref, first_ref, second_ref, row_ref,
    first_t_ref, second_t_ref, col_ref, edge_ref, att_ref, den_ref, carry_ref, halo_ref,
    num_ref, one_ref, two_ref, three_ref, send_sem, recv_sem,
):
    count = q_ref.shape[0]
    lane = lax.broadcasted_iota(jnp.int32, (1, LANES), 1)
    rows, cols = row_ref[...], col_ref[...]
    greet_ring(ring)
    halo = [pass_along(edge_ref, halo_ref, 1, send_sem.at[0, 0], recv_sem.at[0, 0])]

    def local_state(head, none):
        kt = kt_ref[pl.ds(pl.multiple_of(head * FEAT, FEAT), FEAT), :]
        one = dot_nn(first_t_ref[...], kt) + cols[:, 0:1]
        two = dot_nn(second_t_ref[...], kt) + cols[:, 1:2]
        phi = (one * two * cols[:, 2:3] * fresh_ref[...]).astype(bf16)
        put_state(one_ref, head, dot_nn(phi, v_ref[head]))
        return none

    lax.fori_loop(0, HALF_HEADS, local_state, 0)

    def within(head, none):
        mine = (lane // FEAT == head).astype(bf16)
        for i in range(count // TILE):
            at = slice(i * TILE, (i + 1) * TILE)
            q = q_ref[at, :] * mine
            num = jnp.zeros((TILE, LANES), f32)
            for j in range(i + 1):
                to = slice(j * TILE, (j + 1) * TILE)
                dots = dot_nn(q, kt_ref[:, to]) * FEAT**-0.5 + 1.0
                score = (0.5 * dots * dots + 0.5) * allow_ref[at, to].astype(f32)
                num = num + dot_nn(score.astype(bf16), v_ref[head, to, :])
            num_ref[head, at, :] = num
        return none

    copies = exchange(one_ref, two_ref, send_sem.at[0], recv_sem.at[0])
    lax.fori_loop(0, HALF_HEADS // 2, within, 0)
    arrive(copies)
    linked(two_ref, link_ref, three_ref, False)
    back = exchange(three_ref, carry_ref, send_sem.at[1], recv_sem.at[1])
    lax.fori_loop(HALF_HEADS // 2, HALF_HEADS, within, 0)
    arrive(back)
    den_ref[...] = jnp.zeros_like(den_ref)

    def finish(head, none):
        mine = (lane // FEAT == head).astype(bf16)
        carry = get_state(carry_ref, head)
        for i in range(count // TILE):
            at = slice(i * TILE, (i + 1) * TILE)
            q = q_ref[at, :] * mine
            phi = (dot_nn(q, first_ref[...]) + rows[0:1]) * (dot_nn(q, second_ref[...]) + rows[1:2])
            num = num_ref[head, at, :] + dot_nn(phi.astype(bf16), carry) * on_ref[at, :]
            den = num[:, HEAD_WIDTH : HEAD_WIDTH + 1] + 1.0
            att_ref[head, at, :] = (num / den).astype(bf16)
            den_ref[at, :] += jnp.where(lane == head, den, 0.0)
        return none

    lax.fori_loop(0, HALF_HEADS, finish, 0)
    arrive(halo)
    leave(copies + back + halo)


def attend_back_kernel(
    ring, after, link_ref, q_ref, k_ref, qt_ref, kt_ref, v_ref, up_ref, att_ref, den_ref, carry_ref, allow_ref,
    on_ref, on_row_ref, fresh_ref, first_ref, second_ref, row_ref, first_t_ref, second_t_ref, col_ref, edge_ref, *refs,
):
    dq_ref, dk_ref, dv_ref, halo_ref = refs[after : after + 4]
    a_ref, dvs_ref, one_ref, two_ref, three_ref, later_ref, send_sem, recv_sem = refs[after + 4 :]
    count = q_ref.shape[0]
    tiles = count // TILE
    lane = lax.broadcasted_iota(jnp.int32, (1, LANES), 1)
    rows, cols = row_ref[...], col_ref[...]
    first, second = first_ref[...], second_ref[...]
    greet_ring(ring)
    halo = [pass_along(edge_ref, halo_ref, -1, send_sem.at[0, 0], recv_sem.at[0, 0])]
    dq_ref[...] = jnp.zeros_like(dq_ref)
    dk_ref[...] = jnp.zeros_like(dk_ref)

    def query_state(head, none):
        den = jnp.sum(jnp.where(lane == head, den_ref[...], 0.0), axis=1, keepdims=True)
        g = jnp.where(lane < HEAD_WIDTH, up_ref[head].astype(f32) / den, 0.0)
        back = jnp.sum(g * att_ref[head].astype(f32), axis=1, keepdims=True)
        a = jnp.where(lane == HEAD_WIDTH, -back, g).astype(bf16)
        a_ref[head] = a
        qt = qt_ref[pl.ds(pl.multiple_of(head * FEAT, FEAT), FEAT), :]
        one = dot_nn(first_t_ref[...], qt) + cols[:, 0:1]
        two = dot_nn(second_t_ref[...], qt) + cols[:, 1:2]
        phi = (one * two * on_row_ref[...]).astype(bf16)
        put_state(one_ref, head, dot_nn(phi, a))
        return none

    lax.fori_loop(0, HALF_HEADS, query_state, 0)

    def through(vec, d_phi):
        one = dot_nn(vec, first) + rows[0:1]
        two = dot_nn(vec, second) + rows[1:2]
        grad = dot_nt((d_phi * two).astype(bf16), first) + dot_nt((d_phi * one).astype(bf16), second)
        return grad, one * two

    def within(head, none):
        here = lane // FEAT == head
        mine = here.astype(bf16)
        carry = get_state(carry_ref, head)
        q = [q_ref[i * TILE : (i + 1) * TILE, :] * mine for i in range(tiles)]
        k = [k_ref[i * TILE : (i + 1) * TILE, :] * mine for i in range(tiles)]
        dk, dv = [None] * tiles, [None] * tiles
        for i in reversed(range(tiles)):
            at = slice(i * TILE, (i + 1) * TILE)
            a = a_ref[head, at, :]
            dq = through(q[i], dot_nt(a, carry) * on_ref[at, :])[0]
            for j in range(i + 1):
                to = slice(j * TILE, (j + 1) * TILE)
                allow = allow_ref[at, to].astype(f32)
                dots = dot_nn(q[i], kt_ref[:, to]) * FEAT**-0.5 + 1.0
                score = ((0.5 * dots * dots + 0.5) * allow).astype(bf16)
                d_dots = dot_nt(a, v_ref[head, to, :]) * dots * allow * FEAT**-0.5
                d_dots = d_dots.astype(bf16)
                dq = dq + dot_nn(d_dots, k[j])
                dk_more, dv_more = dot_tn(d_dots, q[i]), dot_tn(score, a)
                dk[j] = dk_more if dk[j] is None else dk[j] + dk_more
                dv[j] = dv_more if dv[j] is None else dv[j] + dv_more
            dq_ref[at, :] += jnp.where(here, dq, 0.0)
        for j in range(tiles):
            to = slice(j * TILE, (j + 1) * TILE)
            dk_ref[to, :] += jnp.where(here, dk[j], 0.0)
            dvs_ref[head, to, :] = dv[j]
        return none

    copies = exchange(one_ref, two_ref, send_sem.at[0], recv_sem.at[0])
    lax.fori_loop(0, HALF_HEADS // 2, within, 0)
    arrive(copies)
    linked(two_ref, link_ref, three_ref, True)
    back = exchange(three_ref, later_ref, send_sem.at[1], recv_sem.at[1])
    lax.fori_loop(HALF_HEADS // 2, HALF_HEADS, within, 0)
    arrive(back)

    def finish(head, none):
        here = lane // FEAT == head
        mine = here.astype(bf16)
        later = get_state(later_ref, head)
        for i in range(tiles):
            at = slice(i * TILE, (i + 1) * TILE)
            d_phi = dot_nt(v_ref[head, at, :], later) * rows[2:3] * fresh_ref[at, :]
            grad, phi = through(k_ref[at, :] * mine, d_phi)
            dk_ref[at, :] += jnp.where(here, grad, 0.0)
            phi = (phi * rows[2:3] * fresh_ref[at, :]).astype(bf16)
            dv_ref[head, at, :] = (dvs_ref[head, at, :] + dot_nn(phi, later)).astype(bf16)
        return none

    lax.fori_loop(0, HALF_HEADS, finish, 0)
    arrive(halo)
    leave(copies + back + halo)


def state_blocks(ring):
    return (ring, HALF_HEADS * PHI // ring, LANES)


def attend(link, q, kt, values, allow, on_col, fresh_row, edge, tables, ring):
    count = q.shape[0]
    vmem, smem = pl.BlockSpec(memory_space=pltpu.VMEM), pl.BlockSpec(memory_space=pltpu.SMEM)
    blocks = state_blocks(ring)
    return pl.pallas_call(
        functools.partial(attend_kernel, ring),
        in_specs=[smem] + [vmem] * 13,
        out_specs=[vmem] * 4,
        out_shape=[
            jax.ShapeDtypeStruct((HALF_HEADS, count, LANES), bf16),
            jax.ShapeDtypeStruct((count, LANES), f32),
            jax.ShapeDtypeStruct(blocks, bf16),
            jax.ShapeDtypeStruct(edge.shape, edge.dtype),
        ],
        scratch_shapes=[
            pltpu.VMEM((HALF_HEADS, count, LANES), f32),
            pltpu.VMEM(blocks, bf16),
            pltpu.VMEM(blocks, bf16),
            pltpu.VMEM(blocks, bf16),
            pltpu.SemaphoreType.DMA((2, ring)),
            pltpu.SemaphoreType.DMA((2, ring)),
        ],
        compiler_params=pltpu.CompilerParams(collective_id=3, has_side_effects=True, vmem_limit_bytes=VMEM_LIMIT),
        name="attend",
    )(link, q, kt, values, allow, on_col, fresh_row, tables["first"], tables["second"], tables["rows"],
      tables["first_t"], tables["second_t"], tables["cols"], edge)


def attend_back(link, q, k, qt, kt, values, upstream, att, den, carry, allow, on_col, on_row, fresh_col, edge, tables, ring, after):
    count = q.shape[0]
    vmem, smem = pl.BlockSpec(memory_space=pltpu.VMEM), pl.BlockSpec(memory_space=pltpu.SMEM)
    blocks = state_blocks(ring)
    return pl.pallas_call(
        functools.partial(attend_back_kernel, ring, len(after)),
        in_specs=[smem] + [vmem] * 20 + [pl.BlockSpec(memory_space=pl.ANY)] * len(after),
        out_specs=[vmem] * 4,
        out_shape=[
            jax.ShapeDtypeStruct((count, LANES), f32),
            jax.ShapeDtypeStruct((count, LANES), f32),
            jax.ShapeDtypeStruct((HALF_HEADS, count, LANES), bf16),
            jax.ShapeDtypeStruct(edge.shape, edge.dtype),
        ],
        scratch_shapes=[
            pltpu.VMEM((HALF_HEADS, count, LANES), bf16),
            pltpu.VMEM((HALF_HEADS, count, LANES), f32),
            pltpu.VMEM(blocks, bf16),
            pltpu.VMEM(blocks, bf16),
            pltpu.VMEM(blocks, bf16),
            pltpu.VMEM(blocks, bf16),
            pltpu.SemaphoreType.DMA((2, ring)),
            pltpu.SemaphoreType.DMA((2, ring)),
        ],
        compiler_params=pltpu.CompilerParams(collective_id=4, has_side_effects=True, vmem_limit_bytes=VMEM_LIMIT),
        name="attend_back",
    )(link, q, k, qt, kt, values, upstream, att, den, carry, allow, on_col, on_row, fresh_col,
      tables["first"], tables["second"], tables["rows"], tables["first_t"], tables["second_t"], tables["cols"], edge,
      *after)


def make_tables():
    first, second, bias, scale = feature_tables()
    rows = np.concatenate([bias, scale[None]], axis=0)
    return {
        "first": jnp.asarray(np.tile(first, (HALF_HEADS, 1)), bf16),
        "second": jnp.asarray(np.tile(second, (HALF_HEADS, 1)), bf16),
        "first_t": jnp.asarray(first.T, bf16),
        "second_t": jnp.asarray(second.T, bf16),
        "rows": jnp.asarray(rows, f32),
        "cols": jnp.asarray(rows.T, f32),
    }


def row_major(array):
    return with_layout_constraint(array, Layout(major_to_minor=tuple(range(array.ndim))))


def swap(block):
    return lax.ppermute(block, "core", [(0, 1), (1, 0)])


def in_order(core, mine, theirs):
    return jnp.stack([jnp.where(core == 0, mine, theirs), jnp.where(core == 0, theirs, mine)])


def choose(core, zero, one):
    return jnp.where(core == 0, zero, one)


def tie(block, after):
    if after is None:
        return block
    zero = lax.slice(after, (0,) * after.ndim, (1,) * after.ndim).reshape((1,) * block.ndim) * 0
    return block + zero.astype(block.dtype)


class Halving:
    def __init__(self, parts, orders):
        ring, groups = lax.axis_size("ring"), lax.axis_size("fsdp")
        ring_bits, group_bits = bits_of(ring), bits_of(groups)
        self.place = {("ring", b): ring_bits - 1 - b for b in range(ring_bits)}
        self.place.update({("fsdp", b): ring_bits + group_bits - 1 - b for b in range(group_bits)})
        self.index = {axis: lax.axis_index(axis) for axis in ("ring", "fsdp")}
        shape = (2,) * (ring_bits + group_bits)
        self.parts = [[part.reshape(shape + part.shape[2:])] for part in parts]
        self.orders = orders
        self.at = 0

    def step(self, after=None):
        sent, self.got = [], []
        for which, order in enumerate(self.orders):
            axis, bit = order[self.at]
            dim = self.place[axis, bit]
            mine = (self.index[axis] >> bit) & 1

            def half(term, side):
                return lax.dynamic_slice_in_dim(term, side, 1, axis=dim)

            terms = self.parts[which]
            send = functools.reduce(jnp.add, [half(t, 1 - mine).astype(f32) for t in terms]).astype(bf16)
            send = tie(send, after)
            size = lax.axis_size(axis)
            got = lax.ppermute(send, axis, [(i, i ^ (1 << bit)) for i in range(size)])
            self.parts[which] = [half(t, mine) for t in terms] + [got]
            sent.append(send)
            self.got.append(got)
        self.at += 1
        return sent

    def rest(self):
        found = []
        for terms, order in zip(self.parts, self.orders):
            gone = [self.place[key] for key in order[: self.at]]
            total = functools.reduce(jnp.add, [t.astype(f32) for t in terms]).astype(bf16)
            left = total.reshape([n for dim, n in enumerate(total.shape) if dim not in gone])
            keys = sorted(order[self.at :], key=self.place.get)
            found.append((left, keys, order[self.at :]))
        return found


    def result(self):
        while self.at < len(self.orders[0]):
            self.step()
        totals = []
        for terms in self.parts:
            total = functools.reduce(jnp.add, [t.astype(f32) for t in terms])
            totals.append(total.reshape(total.shape[-2:]))
        return jnp.concatenate(totals, axis=-1)


def both_orders(ring, groups):
    ring_bits = [("ring", b) for b in range(ring.bit_length() - 1)]
    group_bits = [("fsdp", b) for b in reversed(range(groups.bit_length() - 1))]
    near, far = ring_bits[:1], ring_bits[1:]
    return near + group_bits + far, group_bits + near + far


def norm_scale(values, gain):
    return values * lax.rsqrt(jnp.mean(values * values, axis=-1, keepdims=True) + norm_eps) * gain


def segment_ends(lengths_row, order_row):
    count = lengths_row.shape[0]
    picks = order_row[:, None] == jnp.arange(count, dtype=jnp.int32)[None, :]
    ordered = jnp.sum(jnp.where(picks, lengths_row[None, :], 0), axis=1)
    upto = jnp.arange(count)[:, None] >= jnp.arange(count)[None, :]
    return jnp.sum(jnp.where(upto, ordered[None, :], 0), axis=1)


def segment_of(ends, positions):
    found = jnp.sum((positions[:, None] >= ends[None, :]).astype(jnp.int32), axis=1)
    return jnp.where(positions < 0, -1, found)


def adam_step(weight, first, second, grad, rate, decay):
    momentum = beta_one * first + (1.0 - beta_one) * grad
    variance = beta_two * second + (1.0 - beta_two) * grad * grad
    corrected = momentum / (1.0 - beta_one**STEP)
    scaled = variance / (1.0 - beta_two**STEP)
    return (
        weight - rate * (corrected / (jnp.sqrt(scaled) + adam_eps) + decay * weight),
        momentum,
        variance,
    )


def short_conv(extended, taps, same):
    count = same[0].shape[0]
    result = 0.0
    for shift_by in range(3):
        piece = lax.slice_in_dim(extended, 2 - shift_by, 2 - shift_by + count, axis=0)
        result = result + taps[shift_by][None, :] * piece * same[shift_by]
    return result


def per_device(
    hidden_in, cotangent, mixer_weight, output_weight, updown_weight, down_weight, gain_weight,
    mixer_first, output_first, updown_first, down_first, gain_first,
    mixer_second, output_second, updown_second, down_second, gain_second,
    lengths, seq_order, pad_mask,
):
    ring, groups = lax.axis_size("ring"), lax.axis_size("fsdp")
    ring_id, core = lax.axis_index("ring"), lax.axis_index("core")
    local_rows = hidden_in.shape[1]
    count = 2 * local_rows
    qk_cols = HEADS * FEAT
    half_d, half_qk = D // 2, qk_cols // 2
    d_rows, f_rows = mixer_weight.shape[0], down_weight.shape[0]
    pair_ff = 2 * FF // (2 * ring) // 2
    tables = make_tables()

    def gather(block):
        return lax.all_gather(block, ("ring", "fsdp"), axis=0, tiled=False)

    def to_owner(array):
        blocks = array.reshape(array.shape[:-1] + (ring, 2, groups, d_rows))
        return row_major(blocks.swapaxes(-3, -2).reshape(array.shape))

    def from_owner(array):
        blocks = array.reshape(array.shape[:-1] + (ring, groups, 2, d_rows))
        return row_major(blocks.swapaxes(-3, -2).reshape(array.shape))

    def exchanged(halves):
        return in_order(core, choose(core, *halves), swap(choose(core, *halves[::-1])))

    def column_half(weight, c):
        pieces, at = [], 0
        for width in (qk_cols, qk_cols, D, D, D):
            pieces.append(weight[:, at + c * width // 2 : at + (c + 1) * width // 2])
            at += width
        return jnp.concatenate(pieces, axis=1)

    gain_low = jnp.pad(gain_weight.astype(bf16), ((0, 0), (0, LANES - gain_weight.shape[1])))
    mixer_low = mixer_weight.astype(bf16)
    halves = [jnp.concatenate([column_half(mixer_low, c), gain_low], axis=1) for c in range(2)]
    packed = exchanged(halves).reshape(1, 2 * d_rows, -1)
    updown_low = updown_weight.astype(bf16).reshape(d_rows, 2, ring, 2, pair_ff)
    packed_gate, packed_up = [
        exchanged([updown_low[:, which, :, c].reshape(d_rows, FF // 2) for c in range(2)]) for which in range(2)
    ]
    output_low = to_owner(output_weight.astype(bf16))
    packed_output = exchanged([output_low[:, :half_d], output_low[:, half_d:]])
    gate_w = gather(packed_gate).reshape(D, FF // 2)
    mixer_all, output_w = gather_rows(
        [tie(packed, packed_gate), packed_output],
        [[256, 256] + [512] * 4 + [256, 256], [512, 384]],
        [1],
        ring,
        groups,
    )
    mixer_w, gains = mixer_all[:, : 2 * half_qk + 3 * half_d], mixer_all[:, 2 * half_qk + 3 * half_d :].astype(f32)
    up_w = gather(tie(packed_up, mixer_all)).reshape(D, FF // 2)

    hidden_own, upstream_own = to_owner(hidden_in[0]), to_owner(cotangent[0])
    tokens = in_order(core, hidden_own, swap(hidden_own)).reshape(count, D).astype(f32)
    upstream = in_order(core, upstream_own, swap(upstream_own)).reshape(count, D)

    ends = segment_ends(lengths[0], seq_order[0])
    start = ring_id * count
    segment = segment_of(ends, start + jnp.arange(-2, count, dtype=jnp.int32))
    seg = segment[2:]
    keep = lax.dynamic_slice_in_dim(pad_mask[0], start, count).astype(f32)
    tails = segment_of(ends, jnp.arange(1, ring + 1, dtype=jnp.int32) * count - 1)
    on = (seg == segment[1]).astype(f32)
    fresh = jnp.where(seg == seg[count - 1], keep, 0.0)
    row_ids = lax.broadcasted_iota(jnp.int32, (count, count), 0)
    col_ids = lax.broadcasted_iota(jnp.int32, (count, count), 1)
    allow = jnp.where((seg[:, None] == seg[None, :]) & (col_ids <= row_ids), keep[None, :], 0.0).astype(bf16)
    same = [(segment[2 - s : 2 - s + count] == seg).astype(f32)[:, None] for s in range(3)]
    before = jnp.concatenate([jnp.full((1,), -1, jnp.int32), tails[:-1]])
    chips = jnp.arange(ring)
    link = ((before[:, None] == tails[None, :]) & (chips[None, :] < chips[:, None])).astype(f32)

    def per_head(block):
        wide = block.reshape(count, HALF_HEADS, HEAD_WIDTH).transpose(1, 0, 2)
        return jnp.pad(wide, ((0, 0), (0, 0), (0, LANES - HEAD_WIDTH)))

    def from_heads(block):
        return block[:, :, :HEAD_WIDTH].transpose(1, 0, 2).reshape(count, half_d)

    normed_f, norm1_back = jax.vjp(norm_scale, tokens, gains[:, 0])
    normed = normed_f.astype(bf16)
    proj = jnp.dot(normed, mixer_w, preferred_element_type=f32)
    down_w = gather(tie(to_owner(down_weight.astype(bf16)), proj)).reshape(FF // 2, D)
    query = proj[:, :half_qk].astype(bf16)
    key_vecs = proj[:, half_qk : 2 * half_qk].astype(bf16)
    value = proj[:, 2 * half_qk : 2 * half_qk + half_d].astype(bf16)
    conv_in = proj[:, 2 * half_qk + half_d : 2 * half_qk + 2 * half_d].astype(bf16)
    gate = proj[:, 2 * half_qk + 2 * half_d :]
    key_t = key_vecs.T
    lane = jnp.arange(LANES)
    values = jnp.where(lane == HEAD_WIDTH, jnp.ones((), bf16), per_head(value))
    att, den, carry, halo = attend(
        link, tie(query, gate_w), key_t, values, allow, on[:, None], fresh[None, :], conv_in[count - 16 :],
        tables, ring,
    )
    halo = jnp.where(ring_id == 0, jnp.zeros((), bf16), halo[14:])
    extended = jnp.concatenate([halo, conv_in], axis=0).astype(f32)
    taps = lax.dynamic_slice_in_dim(from_owner(gains[:, 2:5].T), core * half_d, half_d, axis=1)

    def gating(ext_in, taps_in, gate_in):
        return short_conv(ext_in, taps_in, same) * jax.nn.sigmoid(gate_in)

    gated, gate_back = jax.vjp(gating, extended, taps, gate)
    mix_half = (from_heads(att).astype(f32) + gated).astype(bf16)
    mix_other = swap(mix_half)
    output_half = lax.dynamic_slice_in_dim(output_w, core * half_d, half_d, axis=0)
    output_other = lax.dynamic_slice_in_dim(output_w, (1 - core) * half_d, half_d, axis=0)
    branch = dot_nn(mix_half, output_half) + dot_nn(mix_other, output_other)
    middle = tokens + branch
    normed2_f, norm2_back = jax.vjp(norm_scale, middle, gains[:, 1])
    normed2 = normed2_f.astype(bf16)
    gate_in, up_in = dot_nn(normed2, gate_w), dot_nn(normed2, up_w)

    def swiglu(gate_part, up_part):
        return jax.nn.silu(gate_part) * up_part

    inner_f, inner_back = jax.vjp(swiglu, gate_in, up_in)
    inner = inner_f.astype(bf16)
    feed_part = jnp.dot(inner, down_w, preferred_element_type=f32)

    def own_rows(block):
        return lax.dynamic_slice_in_dim(block, core * local_rows, local_rows, axis=0)

    def other_rows(block):
        return lax.dynamic_slice_in_dim(block, (1 - core) * local_rows, local_rows, axis=0)

    def by_owner(grad, rows):
        blocks = grad.reshape(ring, groups, rows, grad.shape[-1])
        return jnp.pad(blocks, ((0, 0), (0, 0), (0, -rows % 16), (0, 0)))

    def inner_dot(left_mat, right_mat):
        return dot_tn(left_mat, right_mat).astype(bf16)

    orders = both_orders(ring, groups)

    def column_parts(left_mat, right_mat, rows):
        cut = right_mat.shape[1] // 2
        return [by_owner(inner_dot(left_mat, part), rows) for part in (right_mat[:, :cut], right_mat[:, cut:])]

    down_chain = Halving(column_parts(inner, upstream, f_rows), orders)
    down_chain.step()
    upstream_after = upstream
    for one in down_chain.step():
        upstream_after = tie(upstream_after, one)
    inner_grad = dot_nt(upstream_after, down_w).astype(bf16)
    gate_part_grad, up_part_grad = [g.astype(bf16) for g in inner_back(inner_grad.astype(f32))]
    updown_parts = [by_owner(inner_dot(normed2, g), 2 * d_rows) for g in (gate_part_grad, up_part_grad)]
    updown_chain = Halving(updown_parts, orders)
    updown_sent = updown_chain.step()
    for one in updown_sent + down_chain.step(updown_sent[1]):
        gate_part_grad = tie(gate_part_grad, one)
    normed2_part = (dot_nt(gate_part_grad, gate_w) + dot_nt(up_part_grad, up_w)).astype(bf16)
    normed2_grad = normed2_part.astype(f32) + swap(normed2_part).astype(f32)
    middle_part, gain2_grad = norm2_back(normed2_grad)
    middle_grad = upstream.astype(f32) + middle_part
    branch_grad = middle_grad.astype(bf16)
    output_part = inner_dot(mix_half, branch_grad).reshape(ring // 2, 2, groups * d_rows, D)
    output_keep = lax.dynamic_index_in_dim(output_part, core, axis=1, keepdims=False)
    output_send = lax.dynamic_index_in_dim(output_part, 1 - core, axis=1, keepdims=False)
    output_part = in_order(core, output_keep, swap(output_send)).reshape(ring, groups, d_rows, D)
    output_part = jnp.concatenate([output_part[..., :half_d], output_part[..., half_d:]], axis=2)
    output_part = by_owner(output_part.reshape(D, half_d), 2 * d_rows)
    mix_grad = dot_nt(branch_grad, output_half).astype(bf16)
    ext_grad, taps_grad, gate_grad = gate_back(mix_grad.astype(f32))
    query_g, key_g, value_g, after = attend_back(
        link, query, key_vecs, query.T, key_t, values, per_head(mix_grad), att, den, carry, allow, on[:, None],
        on[None, :], fresh[:, None], ext_grad[:8], tables, ring, [],
    )
    sent = updown_chain.step(key_g) + down_chain.step(key_g)
    after = jnp.where(ring_id == ring - 1, 0.0, after[:2])
    conv_grad = ext_grad[2:] + jnp.pad(after, ((count - 2, 0), (0, 0)))
    proj_grad = jnp.concatenate(
        [
            query_g.astype(bf16), key_g.astype(bf16), from_heads(value_g),
            conv_grad.astype(bf16), gate_grad.astype(bf16),
        ],
        axis=1,
    )
    for one in sent:
        proj_grad = tie(proj_grad, one)
    mixer_part = by_owner(inner_dot(normed, proj_grad), 2 * d_rows)
    normed_part = dot_nt(proj_grad, mixer_w)
    normed_grad = own_rows(normed_part) + swap(other_rows(normed_part))
    tokens_own = own_rows(tokens)
    ignored, norm1_back_own = jax.vjp(norm_scale, tokens_own, gains[:, 0])
    input_part, gain1_grad = norm1_back_own(normed_grad)
    input_grad = from_owner(own_rows(middle_grad) + input_part)

    keys = sorted(updown_chain.place, key=updown_chain.place.get)

    def by_bits(partial):
        return partial.reshape((2,) * len(keys) + partial.shape[2:])

    arrays, specs, widths = [], [], []

    def add_chains(array, columns, chain_keys, chain_orders, ranks):
        at = 0
        for number, width in enumerate(columns):
            specs.append((len(arrays), at, width, chain_keys, chain_orders[number % len(chain_orders)], ranks[number]))
            at += width
        arrays.append(array)
        widths.append(len(columns))

    for number, (left, left_keys, order) in enumerate(updown_chain.rest()):
        add_chains(left, [FF // 4, FF // 4], left_keys, [order], [number / 2, 1 + number / 2])
    add_chains(by_bits(mixer_part), [512] * 5 + [384], keys, orders, [0.0, 0.0, 1.0, 1.0, 2.0, 2.0])
    add_chains(by_bits(output_part), [512, 384], keys, orders, [3.0, 3.0])
    summed = reduce_rest(arrays, specs)
    wholes = []
    for number in widths:
        wholes.append(jnp.concatenate(summed[:number], axis=1))
        summed = summed[number:]
    updown_sum = jnp.concatenate(wholes[:2], axis=1)
    down_sum = from_owner(down_chain.result()[:f_rows])
    mixer_sum = wholes[2]
    output_sum = from_owner(
        wholes[3][: 2 * d_rows].reshape(2, d_rows, half_d).transpose(1, 0, 2).reshape(d_rows, D)
    )

    feed = own_rows(feed_part) + swap(tie(other_rows(feed_part), key_g))
    middle_own = own_rows(middle)
    layer = from_owner((middle_own + feed).astype(bf16))
    branch_own = own_rows(branch)
    stats = jnp.stack([jnp.sum(middle_own * middle_own), jnp.sum(branch_own * branch_own), jnp.sum(feed * feed)])

    taps_wide = lax.dynamic_update_slice(jnp.zeros((3, D), f32), taps_grad, (0, core * half_d))
    gain_grad = jnp.concatenate([from_owner(jnp.stack([gain1_grad, 0.5 * gain2_grad])), taps_wide], axis=0)

    square = functools.reduce(jnp.add, [jnp.sum(g * g) for g in (mixer_sum, updown_sum, down_sum, output_sum)])
    spots = jnp.arange(D)[None, :]
    numbers = functools.reduce(
        jnp.add, [jnp.where(spots == i, n, 0.0) for i, n in enumerate((square, stats[0], stats[1], stats[2]))]
    )
    sums = sum_everywhere(jnp.concatenate([gain_grad, numbers, jnp.zeros((2, D), f32)], axis=0), ring, groups)
    gain_total = sums[:5]
    total_sq = sums[5, 0] + jnp.sum(gain_total * gain_total)
    stat_sum = sums[5, 1:4]
    place = (ring_id * 2 + core) * groups + lax.axis_index("fsdp")
    gain_sum = lax.dynamic_index_in_dim(
        gain_total.reshape(5, 2 * ring * groups, d_rows), place, axis=1, keepdims=False
    ).T

    def own_whole(summed):
        blocks = summed[: 2 * d_rows].reshape(2, d_rows, summed.shape[-1])
        keep_rows = lax.dynamic_index_in_dim(blocks, core, axis=0, keepdims=False)
        send_rows = lax.dynamic_index_in_dim(blocks, 1 - core, axis=0, keepdims=False)
        return in_order(core, keep_rows, swap(send_rows))

    mixer_own = own_whole(mixer_sum)
    pieces, at = [], 0
    for width in (half_qk, half_qk, half_d, half_d, half_d):
        pieces += [mixer_own[0, :, at : at + width], mixer_own[1, :, at : at + width]]
        at += width
    mixer_own = jnp.concatenate(pieces, axis=1)
    updown_own = own_whole(updown_sum).reshape(2, d_rows, 2, ring, pair_ff)
    updown_own = updown_own.transpose(1, 2, 3, 0, 4).reshape(d_rows, 2 * FF)
    grad_list = (mixer_own, output_sum, updown_own, down_sum, gain_sum)
    grad_norm = jnp.sqrt(total_sq)
    factor = jnp.minimum(1.0, clip_level / grad_norm)
    masters = (mixer_weight, output_weight, updown_weight, down_weight, gain_weight)
    firsts = (mixer_first, output_first, updown_first, down_first, gain_first)
    seconds = (mixer_second, output_second, updown_second, down_second, gain_second)
    nexts, moms, varis = ([], [], [])
    for index in range(5):
        rate = rate_gain if index == 4 else rate_matrix
        decay = 0.0 if index == 4 else decay_rate
        new_w, new_m, new_v = adam_step(
            masters[index], firsts[index], seconds[index], grad_list[index] * factor, rate, decay
        )
        nexts.append(new_w)
        moms.append(new_m)
        varis.append(new_v)
    layer_rms = jnp.sqrt(stat_sum / (count * ring * groups * D))
    return (layer[None], input_grad[None], *nexts, *moms, *varis, grad_norm, layer_rms)


def solution(mesh):
    shards, groups = mesh.shape["seq"], mesh.shape["fsdp"]
    split = Mesh(mesh.devices.reshape(shards // 2, 2, groups), ("ring", "core", "fsdp"))
    tokens = P("fsdp", ("ring", "core"), None)
    rows = P(("ring", "core", "fsdp"), None)
    pack = P("fsdp", None)
    return jax.shard_map(
        per_device,
        mesh=split,
        in_specs=(tokens,) * 2 + (rows,) * 15 + (pack,) * 3,
        out_specs=(tokens,) * 2 + (rows,) * 15 + (P(), P()),
        check_vma=False,
    )
```

```python
import functools

import jax
import jax.numpy as jnp
import numpy as np
from jax import lax
from jax.experimental import pallas as pl
from jax.experimental.layout import Layout, with_layout_constraint
from jax.experimental.pallas import tpu as pltpu
from jax.sharding import Mesh
from jax.sharding import PartitionSpec as P

D = 1792
HEADS = 16
FEAT = 16
FF = 4096
STEP = 10
HALF_HEADS = HEADS // 2
HEAD_WIDTH = D // HEADS
PHI = 160
LANES = 128
TILE = 256

norm_eps = 1e-06
beta_one = 0.9
beta_two = 0.95
adam_eps = 1e-08
rate_matrix = 0.05
rate_gain = 1.5
decay_rate = 0.1
clip_level = 1.0

bf16 = jnp.bfloat16
f32 = jnp.float32
VMEM_LIMIT = 48 * 1024 * 1024
GATHER_PACE = (-2.0, -1.2, 0.0, 1.1)
REDUCE_PACE = (0.0, 1.5, 2.6, 3.7, 4.8)


def feature_tables():
    first = np.zeros((FEAT, PHI), np.float32)
    second = np.zeros((FEAT, PHI), np.float32)
    bias = np.zeros((2, PHI), np.float32)
    scale = np.zeros((PHI,), np.float32)
    bias[:, 0] = 1.0
    scale[0] = 1.0
    at = 1
    for a in range(FEAT):
        first[a, at] = 1.0
        bias[1, at] = 1.0
        scale[at] = FEAT**-0.5
        at += 1
    for a in range(FEAT):
        for b in range(a, FEAT):
            first[a, at] = 1.0
            second[b, at] = 1.0
            scale[at] = (1.0 if a == b else 2.0) / (2.0 * FEAT)
            at += 1
    return first, second, bias, scale


def dot_nn(a, b):
    return lax.dot_general(a, b, (((1,), (0,)), ((), ())), preferred_element_type=f32)


def dot_tn(a, b):
    return lax.dot_general(a, b, (((0,), (0,)), ((), ())), preferred_element_type=f32)


def dot_nt(a, b):
    return lax.dot_general(a, b, (((1,), (1,)), ((), ())), preferred_element_type=f32)


def bits_of(size):
    return size.bit_length() - 1


def other(axis, bit):
    me = lax.axis_index(axis)
    return {axis: me + (1 - 2 * ((me // 2**bit) % 2)) * 2**bit}


def greet(partners):
    barrier = pltpu.get_barrier_semaphore()
    for partner in partners:
        pl.semaphore_signal(barrier, inc=1, device_id=partner, device_id_type=pl.DeviceIdType.MESH)
    pl.semaphore_wait(barrier, len(partners))


def gather_kernel(ring, groups, parts, orders, count, shared, *refs):
    in_refs, out_refs = refs[:count], refs[count : 2 * count]
    send_sem, recv_sem, own_sem = refs[2 * count :]
    ring_bits, group_bits = bits_of(ring), bits_of(groups)
    every = [("ring", b) for b in reversed(range(ring_bits))] + [("fsdp", b) for b in reversed(range(group_bits))]
    partners = {key: other(*key) for key in every}
    core_partner = other("core", 0)
    greet(list(partners.values()) + [core_partner])
    core = lax.axis_index("core")
    bit = {(axis, b): (lax.axis_index(axis) // 2**b) % 2 for axis, b in every}

    def view(ref, have, columns):
        spots = [slice(None) if key in have else pl.ds(bit[key], 1) for key in every]
        spots.insert(ring_bits, slice(None))
        return ref.at[tuple(spots) + (slice(None), columns)]

    def placed(part):
        index, at, width = parts[part]
        if index not in shared:
            return pl.ds(at, width)
        return pl.ds(pl.multiple_of(core * in_refs[index].shape[-1] + at, LANES), width)

    steps = len(every)
    events = []
    for part in range(len(parts)):
        for step in range(steps):
            late = GATHER_PACE[min(max(step + 4 - steps, 0), 3)]
            events.append((part // 2 + late, part, step))
    copies, owns = {}, []
    for index in range(count):
        everything = slice(None)
        if index in shared:
            columns = in_refs[index].shape[-1]
            everything = pl.ds(pl.multiple_of(core * columns, LANES), columns)
        owns.append(
            pltpu.make_async_copy(in_refs[index], view(out_refs[index], (), everything), own_sem.at[index])
        )
    owned = False
    for _, part, step in sorted(events):
        if step and not owned:
            owned = True
            for own in owns:
                own.start()
            for own in owns:
                own.wait()
        order = orders[part % len(orders)]
        if step:
            copies[part, step - 1].wait_recv()
        index, at, width = parts[part]
        ndim = in_refs[index].ndim
        here = view(out_refs[index], order[:step], placed(part))
        source = in_refs[index].at[(slice(None),) * (ndim - 1) + (pl.ds(at, width),)] if step == 0 else here
        copies[part, step] = pltpu.make_async_remote_copy(
            src_ref=source,
            dst_ref=here,
            send_sem=send_sem.at[part, step],
            recv_sem=recv_sem.at[part, step],
            device_id=partners[order[step]],
            device_id_type=pl.DeviceIdType.MESH,
        )
        copies[part, step].start()
    for part in range(len(parts)):
        copies[part, steps - 1].wait_recv()
        if parts[part][0] in shared:
            here = view(out_refs[parts[part][0]], every, placed(part))
            copies[part, steps] = pltpu.make_async_remote_copy(
                src_ref=here,
                dst_ref=here,
                send_sem=send_sem.at[part, steps],
                recv_sem=recv_sem.at[part, steps],
                device_id=core_partner,
                device_id_type=pl.DeviceIdType.MESH,
            )
            copies[part, steps].start()
    for part in range(len(parts)):
        if parts[part][0] in shared:
            copies[part, steps].wait_recv()
    for copy in copies.values():
        copy.wait_send()


def gather_rows(blocks, cuts, shared, ring, groups):
    ring_bits, group_bits = bits_of(ring), bits_of(groups)
    near, far = [("ring", 0)], [("ring", b) for b in reversed(range(1, ring_bits))]
    group = [("fsdp", b) for b in reversed(range(group_bits))]
    orders = (far + near + group, far + group + near)
    parts = []
    for index, widths in enumerate(cuts):
        at = 0
        for width in widths:
            parts.append((index, at, width))
            at += width
    steps = ring_bits + group_bits
    ins, shapes, size = [], [], 0
    for block in blocks:
        cores, rows, columns = block.shape
        ins.append(block.reshape((1,) * ring_bits + (cores,) + (1,) * group_bits + (rows, columns)))
        width = 2 * columns if len(ins) - 1 in shared else columns
        shape = (2,) * ring_bits + (cores,) + (2,) * group_bits + (rows, width)
        shapes.append(jax.ShapeDtypeStruct(shape, block.dtype))
        size += 2 * block.size * ring * groups
    outs = pl.pallas_call(
        functools.partial(gather_kernel, ring, groups, parts, orders, len(blocks), shared),
        in_specs=[pl.BlockSpec(memory_space=pl.ANY)] * len(blocks),
        out_specs=[pl.BlockSpec(memory_space=pl.ANY)] * len(blocks),
        out_shape=shapes,
        scratch_shapes=[
            pltpu.SemaphoreType.DMA((len(parts), steps + 1)),
            pltpu.SemaphoreType.DMA((len(parts), steps + 1)),
            pltpu.SemaphoreType.DMA((len(blocks),)),
        ],
        compiler_params=pltpu.CompilerParams(collective_id=0, has_side_effects=True),
        cost_estimate=pl.CostEstimate(flops=0, bytes_accessed=20 * size, transcendentals=0),
        name="gather_rows",
    )(*ins)
    return [o.reshape((2 * ring * groups if b.shape[0] == 2 else ring * groups) * b.shape[1], o.shape[-1])
            for o, b in zip(outs, blocks)]


def reduce_kernel(chains, partners, pairs, *refs):
    refs = list(refs)

    def take(number):
        taken = refs[:number]
        del refs[:number]
        return taken

    in_refs, out_refs = take(pairs), take(len(chains))
    own_refs = take(len(chains))
    recv_refs = [take(len(chain[4])) for chain in chains]
    send_refs = [take(len(chain[4]) - 1) for chain in chains]
    send_sem, recv_sem, own_sem = take(3)
    greet([other(*key) for key in partners])
    mine = {(axis, b): (lax.axis_index(axis) // 2**b) % 2 for axis, b in partners}
    copies = {}

    def start(c, step, source):
        copies[c, step] = pltpu.make_async_remote_copy(
            src_ref=source,
            dst_ref=recv_refs[c][step],
            send_sem=send_sem.at[c, step],
            recv_sem=recv_sem.at[c, step],
            device_id=other(*chains[c][4][step]),
            device_id_type=pl.DeviceIdType.MESH,
        )
        copies[c, step].start()

    def first_half(c, side):
        source, at, width, keys, order, rank = chains[c]
        spots = tuple(side if key == order[0] else slice(None) for key in keys)
        return in_refs[source].at[spots + (slice(None), pl.ds(at, width))]

    def add_up(c, step, target):
        keys, order = chains[c][3], chains[c][4]
        left = [key for key in keys if key not in order[: step + 1]]
        rows = target.shape[-2]
        tile = 16 if rows % 16 == 0 else rows
        for spot in np.ndindex(*(2,) * len(left)):
            spot = tuple(int(i) for i in spot)
            free = dict(zip(left, spot))

            def where(key):
                if key in free:
                    return free[key]
                return 1 - mine[key] if step < len(order) and key == order[step] else mine[key]

            def body(i, carry):
                at = pl.ds(pl.multiple_of(i * tile, tile), tile)
                total = None
                for t in range(step + 1):
                    ref = own_refs[c] if t == 0 else recv_refs[c][t - 1]
                    index = tuple(where(key) for key in keys if key not in order[: max(t, 1)])
                    term = ref[index + (at, slice(None))].astype(f32)
                    total = term if total is None else total + term
                target[spot + (at, slice(None))] = total.astype(target.dtype)
                return carry

            lax.fori_loop(0, rows // tile, body, 0)

    owns = []
    for c in range(len(chains)):
        own = pltpu.make_async_copy(first_half(c, mine[chains[c][4][0]]), own_refs[c], own_sem.at[c])
        own.start()
        owns.append(own)
    events = []
    for c, chain in enumerate(chains):
        for step in range(len(chain[4]) + 1):
            events.append((chain[5] + REDUCE_PACE[min(step, 4)], c, step))
    for _, c, step in sorted(events):
        order = chains[c][4]
        if step == 0:
            start(c, 0, first_half(c, 1 - mine[order[0]]))
            continue
        if step == 1:
            owns[c].wait()
        copies[c, step - 1].wait_recv()
        if step < len(order):
            add_up(c, step, send_refs[c][step - 1])
            start(c, step, send_refs[c][step - 1])
        else:
            add_up(c, step, out_refs[c])
    for copy in copies.values():
        copy.wait_send()


def reduce_rest(arrays, specs):
    outs, owns, recvs, sends = [], [], [], []
    steps = 0
    for source, at, width, keys, order, rank in specs:
        rows = arrays[source].shape[-2]
        steps = max(steps, len(order))
        outs.append(jax.ShapeDtypeStruct((rows, width), f32))
        shapes = [(2,) * (len(keys) - step - 1) + (rows, width) for step in range(len(order))]
        owns.append(pltpu.VMEM(shapes[0], bf16))
        recvs += [pltpu.VMEM(shape, bf16) for shape in shapes]
        sends += [pltpu.VMEM(shape, bf16) for shape in shapes[1:]]
    partners = sorted({key for spec in specs for key in spec[4]})
    sems = (len(specs), steps)
    return pl.pallas_call(
        functools.partial(reduce_kernel, specs, partners, len(arrays)),
        in_specs=[pl.BlockSpec(memory_space=pl.ANY)] * len(arrays),
        out_specs=[pl.BlockSpec(memory_space=pltpu.VMEM)] * len(specs),
        out_shape=outs,
        scratch_shapes=owns
        + recvs
        + sends
        + [
            pltpu.SemaphoreType.DMA(sems),
            pltpu.SemaphoreType.DMA(sems),
            pltpu.SemaphoreType.DMA((len(specs),)),
        ],
        compiler_params=pltpu.CompilerParams(
            collective_id=2, has_side_effects=True, vmem_limit_bytes=58 * 1024 * 1024
        ),
        name="reduce_rest",
    )(*arrays)


def sum_kernel(partners, in_ref, out_ref, held, got, send_sem, recv_sem):
    partners = [other(*key) for key in partners]
    greet(partners)
    held[0] = in_ref[...]
    for step, partner in enumerate(partners):
        copy = pltpu.make_async_remote_copy(
            src_ref=held.at[step],
            dst_ref=got.at[step],
            send_sem=send_sem.at[step],
            recv_sem=recv_sem.at[step],
            device_id=partner,
            device_id_type=pl.DeviceIdType.MESH,
        )
        copy.start()
        copy.wait()
        total = held[step] + got[step]
        if step + 1 < len(partners):
            held[step + 1] = total
        else:
            out_ref[...] = total


def sum_everywhere(block, ring, groups):
    partners = [("core", 0)] + [("ring", b) for b in range(bits_of(ring))] + [("fsdp", b) for b in range(bits_of(groups))]
    steps = len(partners)
    return pl.pallas_call(
        functools.partial(sum_kernel, partners),
        in_specs=[pl.BlockSpec(memory_space=pltpu.VMEM)],
        out_specs=pl.BlockSpec(memory_space=pltpu.VMEM),
        out_shape=jax.ShapeDtypeStruct(block.shape, f32),
        scratch_shapes=[
            pltpu.VMEM((steps,) + block.shape, f32),
            pltpu.VMEM((steps,) + block.shape, f32),
            pltpu.SemaphoreType.DMA((steps,)),
            pltpu.SemaphoreType.DMA((steps,)),
        ],
        compiler_params=pltpu.CompilerParams(collective_id=1, has_side_effects=True),
        name="sum_everywhere",
    )(block)


def exchange(source, target, send_sem, recv_sem):
    ring = source.shape[0]
    me = lax.axis_index("ring")
    copies = []
    for away in range(1, ring):
        peer = (me + away) % ring
        copy = pltpu.make_async_remote_copy(
            src_ref=source.at[peer],
            dst_ref=target.at[me],
            send_sem=send_sem.at[away],
            recv_sem=recv_sem.at[away],
            device_id={"ring": peer},
            device_id_type=pl.DeviceIdType.MESH,
        )
        copy.start()
        copies.append(copy)
    target[me] = source[me]
    return copies


def pass_along(source, target, away, send_sem, recv_sem):
    ring = lax.axis_size("ring")
    copy = pltpu.make_async_remote_copy(
        src_ref=source,
        dst_ref=target,
        send_sem=send_sem,
        recv_sem=recv_sem,
        device_id={"ring": (lax.axis_index("ring") + ring + away) % ring},
        device_id_type=pl.DeviceIdType.MESH,
    )
    copy.start()
    return copy


def arrive(copies):
    for copy in copies:
        copy.wait_recv()


def leave(copies):
    for copy in copies:
        copy.wait_send()


def greet_ring(ring):
    me = lax.axis_index("ring")
    greet([{"ring": (me + away) % ring} for away in range(1, ring)])


def put_state(buffer, head, state):
    ring, piece = buffer.shape[0], buffer.shape[1]
    share = ring // HALF_HEADS
    for part in range(share):
        buffer[head * share + part] = state[part * piece : (part + 1) * piece].astype(bf16)


def get_state(buffer, head):
    share = buffer.shape[0] // HALF_HEADS
    if share == 1:
        return buffer[head]
    return jnp.concatenate([buffer[head * share + part] for part in range(share)], axis=0)


def linked(states, link_ref, target, backward):
    ring = states.shape[0]
    for d in range(ring):
        total = jnp.zeros(states.shape[1:], f32)
        for e in range(d + 1, ring) if backward else range(d):
            weight = link_ref[e, d] if backward else link_ref[d, e]
            total = total + weight * states[e].astype(f32)
        target[d] = total.astype(bf16)


def attend_kernel(
    ring, link_ref, q_ref, kt_ref, v_ref, allow_ref, on_ref, fresh_ref, first_ref, second_ref, row_ref,
    first_t_ref, second_t_ref, col_ref, edge_ref, att_ref, den_ref, carry_ref, halo_ref,
    num_ref, one_ref, two_ref, three_ref, send_sem, recv_sem,
):
    count = q_ref.shape[0]
    lane = lax.broadcasted_iota(jnp.int32, (1, LANES), 1)
    rows, cols = row_ref[...], col_ref[...]
    greet_ring(ring)
    halo = [pass_along(edge_ref, halo_ref, 1, send_sem.at[0, 0], recv_sem.at[0, 0])]

    def local_state(head, none):
        kt = kt_ref[pl.ds(pl.multiple_of(head * FEAT, FEAT), FEAT), :]
        one = dot_nn(first_t_ref[...], kt) + cols[:, 0:1]
        two = dot_nn(second_t_ref[...], kt) + cols[:, 1:2]
        phi = (one * two * cols[:, 2:3] * fresh_ref[...]).astype(bf16)
        put_state(one_ref, head, dot_nn(phi, v_ref[head]))
        return none

    lax.fori_loop(0, HALF_HEADS, local_state, 0)

    def within(head, none):
        mine = (lane // FEAT == head).astype(bf16)
        for i in range(count // TILE):
            at = slice(i * TILE, (i + 1) * TILE)
            q = q_ref[at, :] * mine
            num = jnp.zeros((TILE, LANES), f32)
            for j in range(i + 1):
                to = slice(j * TILE, (j + 1) * TILE)
                dots = dot_nn(q, kt_ref[:, to]) * FEAT**-0.5 + 1.0
                score = (0.5 * dots * dots + 0.5) * allow_ref[at, to].astype(f32)
                num = num + dot_nn(score.astype(bf16), v_ref[head, to, :])
            num_ref[head, at, :] = num
        return none

    copies = exchange(one_ref, two_ref, send_sem.at[0], recv_sem.at[0])
    lax.fori_loop(0, HALF_HEADS // 2, within, 0)
    arrive(copies)
    linked(two_ref, link_ref, three_ref, False)
    back = exchange(three_ref, carry_ref, send_sem.at[1], recv_sem.at[1])
    lax.fori_loop(HALF_HEADS // 2, HALF_HEADS, within, 0)
    arrive(back)
    den_ref[...] = jnp.zeros_like(den_ref)

    def finish(head, none):
        mine = (lane // FEAT == head).astype(bf16)
        carry = get_state(carry_ref, head)
        for i in range(count // TILE):
            at = slice(i * TILE, (i + 1) * TILE)
            q = q_ref[at, :] * mine
            phi = (dot_nn(q, first_ref[...]) + rows[0:1]) * (dot_nn(q, second_ref[...]) + rows[1:2])
            num = num_ref[head, at, :] + dot_nn(phi.astype(bf16), carry) * on_ref[at, :]
            den = num[:, HEAD_WIDTH : HEAD_WIDTH + 1] + 1.0
            att_ref[head, at, :] = (num / den).astype(bf16)
            den_ref[at, :] += jnp.where(lane == head, den, 0.0)
        return none

    lax.fori_loop(0, HALF_HEADS, finish, 0)
    arrive(halo)
    leave(copies + back + halo)


def attend_back_kernel(
    ring, after, link_ref, q_ref, k_ref, qt_ref, kt_ref, v_ref, up_ref, att_ref, den_ref, carry_ref, allow_ref,
    on_ref, on_row_ref, fresh_ref, first_ref, second_ref, row_ref, first_t_ref, second_t_ref, col_ref, edge_ref, *refs,
):
    dq_ref, dk_ref, dv_ref, halo_ref = refs[after : after + 4]
    a_ref, dvs_ref, one_ref, two_ref, three_ref, later_ref, send_sem, recv_sem = refs[after + 4 :]
    count = q_ref.shape[0]
    tiles = count // TILE
    lane = lax.broadcasted_iota(jnp.int32, (1, LANES), 1)
    rows, cols = row_ref[...], col_ref[...]
    first, second = first_ref[...], second_ref[...]
    greet_ring(ring)
    halo = [pass_along(edge_ref, halo_ref, -1, send_sem.at[0, 0], recv_sem.at[0, 0])]
    dq_ref[...] = jnp.zeros_like(dq_ref)
    dk_ref[...] = jnp.zeros_like(dk_ref)

    def query_state(head, none):
        den = jnp.sum(jnp.where(lane == head, den_ref[...], 0.0), axis=1, keepdims=True)
        g = jnp.where(lane < HEAD_WIDTH, up_ref[head].astype(f32) / den, 0.0)
        back = jnp.sum(g * att_ref[head].astype(f32), axis=1, keepdims=True)
        a = jnp.where(lane == HEAD_WIDTH, -back, g).astype(bf16)
        a_ref[head] = a
        qt = qt_ref[pl.ds(pl.multiple_of(head * FEAT, FEAT), FEAT), :]
        one = dot_nn(first_t_ref[...], qt) + cols[:, 0:1]
        two = dot_nn(second_t_ref[...], qt) + cols[:, 1:2]
        phi = (one * two * on_row_ref[...]).astype(bf16)
        put_state(one_ref, head, dot_nn(phi, a))
        return none

    lax.fori_loop(0, HALF_HEADS, query_state, 0)

    def through(vec, d_phi):
        one = dot_nn(vec, first) + rows[0:1]
        two = dot_nn(vec, second) + rows[1:2]
        grad = dot_nt((d_phi * two).astype(bf16), first) + dot_nt((d_phi * one).astype(bf16), second)
        return grad, one * two

    def within(head, none):
        here = lane // FEAT == head
        mine = here.astype(bf16)
        carry = get_state(carry_ref, head)
        q = [q_ref[i * TILE : (i + 1) * TILE, :] * mine for i in range(tiles)]
        k = [k_ref[i * TILE : (i + 1) * TILE, :] * mine for i in range(tiles)]
        dk, dv = [None] * tiles, [None] * tiles
        for i in reversed(range(tiles)):
            at = slice(i * TILE, (i + 1) * TILE)
            a = a_ref[head, at, :]
            dq = through(q[i], dot_nt(a, carry) * on_ref[at, :])[0]
            for j in range(i + 1):
                to = slice(j * TILE, (j + 1) * TILE)
                allow = allow_ref[at, to].astype(f32)
                dots = dot_nn(q[i], kt_ref[:, to]) * FEAT**-0.5 + 1.0
                score = ((0.5 * dots * dots + 0.5) * allow).astype(bf16)
                d_dots = dot_nt(a, v_ref[head, to, :]) * dots * allow * FEAT**-0.5
                d_dots = d_dots.astype(bf16)
                dq = dq + dot_nn(d_dots, k[j])
                dk_more, dv_more = dot_tn(d_dots, q[i]), dot_tn(score, a)
                dk[j] = dk_more if dk[j] is None else dk[j] + dk_more
                dv[j] = dv_more if dv[j] is None else dv[j] + dv_more
            dq_ref[at, :] += jnp.where(here, dq, 0.0)
        for j in range(tiles):
            to = slice(j * TILE, (j + 1) * TILE)
            dk_ref[to, :] += jnp.where(here, dk[j], 0.0)
            dvs_ref[head, to, :] = dv[j]
        return none

    copies = exchange(one_ref, two_ref, send_sem.at[0], recv_sem.at[0])
    lax.fori_loop(0, HALF_HEADS // 2, within, 0)
    arrive(copies)
    linked(two_ref, link_ref, three_ref, True)
    back = exchange(three_ref, later_ref, send_sem.at[1], recv_sem.at[1])
    lax.fori_loop(HALF_HEADS // 2, HALF_HEADS, within, 0)
    arrive(back)

    def finish(head, none):
        here = lane // FEAT == head
        mine = here.astype(bf16)
        later = get_state(later_ref, head)
        for i in range(tiles):
            at = slice(i * TILE, (i + 1) * TILE)
            d_phi = dot_nt(v_ref[head, at, :], later) * rows[2:3] * fresh_ref[at, :]
            grad, phi = through(k_ref[at, :] * mine, d_phi)
            dk_ref[at, :] += jnp.where(here, grad, 0.0)
            phi = (phi * rows[2:3] * fresh_ref[at, :]).astype(bf16)
            dv_ref[head, at, :] = (dvs_ref[head, at, :] + dot_nn(phi, later)).astype(bf16)
        return none

    lax.fori_loop(0, HALF_HEADS, finish, 0)
    arrive(halo)
    leave(copies + back + halo)


def state_blocks(ring):
    return (ring, HALF_HEADS * PHI // ring, LANES)


def attend(link, q, kt, values, allow, on_col, fresh_row, edge, tables, ring):
    count = q.shape[0]
    vmem, smem = pl.BlockSpec(memory_space=pltpu.VMEM), pl.BlockSpec(memory_space=pltpu.SMEM)
    blocks = state_blocks(ring)
    return pl.pallas_call(
        functools.partial(attend_kernel, ring),
        in_specs=[smem] + [vmem] * 13,
        out_specs=[vmem] * 4,
        out_shape=[
            jax.ShapeDtypeStruct((HALF_HEADS, count, LANES), bf16),
            jax.ShapeDtypeStruct((count, LANES), f32),
            jax.ShapeDtypeStruct(blocks, bf16),
            jax.ShapeDtypeStruct(edge.shape, edge.dtype),
        ],
        scratch_shapes=[
            pltpu.VMEM((HALF_HEADS, count, LANES), f32),
            pltpu.VMEM(blocks, bf16),
            pltpu.VMEM(blocks, bf16),
            pltpu.VMEM(blocks, bf16),
            pltpu.SemaphoreType.DMA((2, ring)),
            pltpu.SemaphoreType.DMA((2, ring)),
        ],
        compiler_params=pltpu.CompilerParams(collective_id=3, has_side_effects=True, vmem_limit_bytes=VMEM_LIMIT),
        name="attend",
    )(link, q, kt, values, allow, on_col, fresh_row, tables["first"], tables["second"], tables["rows"],
      tables["first_t"], tables["second_t"], tables["cols"], edge)


def attend_back(link, q, k, qt, kt, values, upstream, att, den, carry, allow, on_col, on_row, fresh_col, edge, tables, ring, after):
    count = q.shape[0]
    vmem, smem = pl.BlockSpec(memory_space=pltpu.VMEM), pl.BlockSpec(memory_space=pltpu.SMEM)
    blocks = state_blocks(ring)
    return pl.pallas_call(
        functools.partial(attend_back_kernel, ring, len(after)),
        in_specs=[smem] + [vmem] * 20 + [pl.BlockSpec(memory_space=pl.ANY)] * len(after),
        out_specs=[vmem] * 4,
        out_shape=[
            jax.ShapeDtypeStruct((count, LANES), f32),
            jax.ShapeDtypeStruct((count, LANES), f32),
            jax.ShapeDtypeStruct((HALF_HEADS, count, LANES), bf16),
            jax.ShapeDtypeStruct(edge.shape, edge.dtype),
        ],
        scratch_shapes=[
            pltpu.VMEM((HALF_HEADS, count, LANES), bf16),
            pltpu.VMEM((HALF_HEADS, count, LANES), f32),
            pltpu.VMEM(blocks, bf16),
            pltpu.VMEM(blocks, bf16),
            pltpu.VMEM(blocks, bf16),
            pltpu.VMEM(blocks, bf16),
            pltpu.SemaphoreType.DMA((2, ring)),
            pltpu.SemaphoreType.DMA((2, ring)),
        ],
        compiler_params=pltpu.CompilerParams(collective_id=4, has_side_effects=True, vmem_limit_bytes=VMEM_LIMIT),
        name="attend_back",
    )(link, q, k, qt, kt, values, upstream, att, den, carry, allow, on_col, on_row, fresh_col,
      tables["first"], tables["second"], tables["rows"], tables["first_t"], tables["second_t"], tables["cols"], edge,
      *after)


def make_tables():
    first, second, bias, scale = feature_tables()
    rows = np.concatenate([bias, scale[None]], axis=0)
    return {
        "first": jnp.asarray(np.tile(first, (HALF_HEADS, 1)), bf16),
        "second": jnp.asarray(np.tile(second, (HALF_HEADS, 1)), bf16),
        "first_t": jnp.asarray(first.T, bf16),
        "second_t": jnp.asarray(second.T, bf16),
        "rows": jnp.asarray(rows, f32),
        "cols": jnp.asarray(rows.T, f32),
    }


def row_major(array):
    return with_layout_constraint(array, Layout(major_to_minor=tuple(range(array.ndim))))


def swap(block):
    return lax.ppermute(block, "core", [(0, 1), (1, 0)])


def in_order(core, mine, theirs):
    return jnp.stack([jnp.where(core == 0, mine, theirs), jnp.where(core == 0, theirs, mine)])


def choose(core, zero, one):
    return jnp.where(core == 0, zero, one)


def tie(block, after):
    if after is None:
        return block
    zero = lax.slice(after, (0,) * after.ndim, (1,) * after.ndim).reshape((1,) * block.ndim) * 0
    return block + zero.astype(block.dtype)


class Halving:
    def __init__(self, parts, orders):
        ring, groups = lax.axis_size("ring"), lax.axis_size("fsdp")
        ring_bits, group_bits = bits_of(ring), bits_of(groups)
        self.place = {("ring", b): ring_bits - 1 - b for b in range(ring_bits)}
        self.place.update({("fsdp", b): ring_bits + group_bits - 1 - b for b in range(group_bits)})
        self.index = {axis: lax.axis_index(axis) for axis in ("ring", "fsdp")}
        shape = (2,) * (ring_bits + group_bits)
        self.parts = [[part.reshape(shape + part.shape[2:])] for part in parts]
        self.orders = orders
        self.at = 0

    def step(self, after=None):
        sent, self.got = [], []
        for which, order in enumerate(self.orders):
            axis, bit = order[self.at]
            dim = self.place[axis, bit]
            mine = (self.index[axis] >> bit) & 1

            def half(term, side):
                return lax.dynamic_slice_in_dim(term, side, 1, axis=dim)

            terms = self.parts[which]
            send = functools.reduce(jnp.add, [half(t, 1 - mine).astype(f32) for t in terms]).astype(bf16)
            send = tie(send, after)
            size = lax.axis_size(axis)
            got = lax.ppermute(send, axis, [(i, i ^ (1 << bit)) for i in range(size)])
            self.parts[which] = [half(t, mine) for t in terms] + [got]
            sent.append(send)
            self.got.append(got)
        self.at += 1
        return sent

    def rest(self):
        found = []
        for terms, order in zip(self.parts, self.orders):
            gone = [self.place[key] for key in order[: self.at]]
            total = functools.reduce(jnp.add, [t.astype(f32) for t in terms]).astype(bf16)
            left = total.reshape([n for dim, n in enumerate(total.shape) if dim not in gone])
            keys = sorted(order[self.at :], key=self.place.get)
            found.append((left, keys, order[self.at :]))
        return found


    def result(self):
        while self.at < len(self.orders[0]):
            self.step()
        totals = []
        for terms in self.parts:
            total = functools.reduce(jnp.add, [t.astype(f32) for t in terms])
            totals.append(total.reshape(total.shape[-2:]))
        return jnp.concatenate(totals, axis=-1)


def both_orders(ring, groups):
    ring_bits = [("ring", b) for b in range(ring.bit_length() - 1)]
    group_bits = [("fsdp", b) for b in reversed(range(groups.bit_length() - 1))]
    near, far = ring_bits[:1], ring_bits[1:]
    return near + group_bits + far, group_bits + near + far


def norm_scale(values, gain):
    return values * lax.rsqrt(jnp.mean(values * values, axis=-1, keepdims=True) + norm_eps) * gain


def segment_ends(lengths_row, order_row):
    count = lengths_row.shape[0]
    picks = order_row[:, None] == jnp.arange(count, dtype=jnp.int32)[None, :]
    ordered = jnp.sum(jnp.where(picks, lengths_row[None, :], 0), axis=1)
    upto = jnp.arange(count)[:, None] >= jnp.arange(count)[None, :]
    return jnp.sum(jnp.where(upto, ordered[None, :], 0), axis=1)


def segment_of(ends, positions):
    found = jnp.sum((positions[:, None] >= ends[None, :]).astype(jnp.int32), axis=1)
    return jnp.where(positions < 0, -1, found)


def adam_step(weight, first, second, grad, rate, decay):
    momentum = beta_one * first + (1.0 - beta_one) * grad
    variance = beta_two * second + (1.0 - beta_two) * grad * grad
    corrected = momentum / (1.0 - beta_one**STEP)
    scaled = variance / (1.0 - beta_two**STEP)
    return (
        weight - rate * (corrected / (jnp.sqrt(scaled) + adam_eps) + decay * weight),
        momentum,
        variance,
    )


def short_conv(extended, taps, same):
    count = same[0].shape[0]
    result = 0.0
    for shift_by in range(3):
        piece = lax.slice_in_dim(extended, 2 - shift_by, 2 - shift_by + count, axis=0)
        result = result + taps[shift_by][None, :] * piece * same[shift_by]
    return result


def per_device(
    hidden_in, cotangent, mixer_weight, output_weight, updown_weight, down_weight, gain_weight,
    mixer_first, output_first, updown_first, down_first, gain_first,
    mixer_second, output_second, updown_second, down_second, gain_second,
    lengths, seq_order, pad_mask,
):
    ring, groups = lax.axis_size("ring"), lax.axis_size("fsdp")
    ring_id, core = lax.axis_index("ring"), lax.axis_index("core")
    local_rows = hidden_in.shape[1]
    count = 2 * local_rows
    qk_cols = HEADS * FEAT
    half_d, half_qk = D // 2, qk_cols // 2
    d_rows, f_rows = mixer_weight.shape[0], down_weight.shape[0]
    pair_ff = 2 * FF // (2 * ring) // 2
    tables = make_tables()

    def gather(block):
        return lax.all_gather(block, ("ring", "fsdp"), axis=0, tiled=False)

    def to_owner(array):
        blocks = array.reshape(array.shape[:-1] + (ring, 2, groups, d_rows))
        return row_major(blocks.swapaxes(-3, -2).reshape(array.shape))

    def from_owner(array):
        blocks = array.reshape(array.shape[:-1] + (ring, groups, 2, d_rows))
        return row_major(blocks.swapaxes(-3, -2).reshape(array.shape))

    def exchanged(halves):
        return in_order(core, choose(core, *halves), swap(choose(core, *halves[::-1])))

    def column_half(weight, c):
        pieces, at = [], 0
        for width in (qk_cols, qk_cols, D, D, D):
            pieces.append(weight[:, at + c * width // 2 : at + (c + 1) * width // 2])
            at += width
        return jnp.concatenate(pieces, axis=1)

    gain_low = jnp.pad(gain_weight.astype(bf16), ((0, 0), (0, LANES - gain_weight.shape[1])))
    mixer_low = mixer_weight.astype(bf16)
    halves = [jnp.concatenate([column_half(mixer_low, c), gain_low], axis=1) for c in range(2)]
    packed = exchanged(halves).reshape(1, 2 * d_rows, -1)
    updown_low = updown_weight.astype(bf16).reshape(d_rows, 2, ring, 2, pair_ff)
    packed_gate, packed_up = [
        exchanged([updown_low[:, which, :, c].reshape(d_rows, FF // 2) for c in range(2)]) for which in range(2)
    ]
    output_low = to_owner(output_weight.astype(bf16))
    packed_output = exchanged([output_low[:, :half_d], output_low[:, half_d:]])
    gate_w = gather(packed_gate).reshape(D, FF // 2)
    mixer_all, output_w = gather_rows(
        [tie(packed, packed_gate), packed_output],
        [[256, 256] + [512] * 4 + [256, 256], [512, 384]],
        [1],
        ring,
        groups,
    )
    mixer_w, gains = mixer_all[:, : 2 * half_qk + 3 * half_d], mixer_all[:, 2 * half_qk + 3 * half_d :].astype(f32)
    up_w = gather(tie(packed_up, mixer_all)).reshape(D, FF // 2)

    hidden_own, upstream_own = to_owner(hidden_in[0]), to_owner(cotangent[0])
    tokens = in_order(core, hidden_own, swap(hidden_own)).reshape(count, D).astype(f32)
    upstream = in_order(core, upstream_own, swap(upstream_own)).reshape(count, D)

    ends = segment_ends(lengths[0], seq_order[0])
    start = ring_id * count
    segment = segment_of(ends, start + jnp.arange(-2, count, dtype=jnp.int32))
    seg = segment[2:]
    keep = lax.dynamic_slice_in_dim(pad_mask[0], start, count).astype(f32)
    tails = segment_of(ends, jnp.arange(1, ring + 1, dtype=jnp.int32) * count - 1)
    on = (seg == segment[1]).astype(f32)
    fresh = jnp.where(seg == seg[count - 1], keep, 0.0)
    row_ids = lax.broadcasted_iota(jnp.int32, (count, count), 0)
    col_ids = lax.broadcasted_iota(jnp.int32, (count, count), 1)
    allow = jnp.where((seg[:, None] == seg[None, :]) & (col_ids <= row_ids), keep[None, :], 0.0).astype(bf16)
    same = [(segment[2 - s : 2 - s + count] == seg).astype(f32)[:, None] for s in range(3)]
    before = jnp.concatenate([jnp.full((1,), -1, jnp.int32), tails[:-1]])
    chips = jnp.arange(ring)
    link = ((before[:, None] == tails[None, :]) & (chips[None, :] < chips[:, None])).astype(f32)

    def per_head(block):
        wide = block.reshape(count, HALF_HEADS, HEAD_WIDTH).transpose(1, 0, 2)
        return jnp.pad(wide, ((0, 0), (0, 0), (0, LANES - HEAD_WIDTH)))

    def from_heads(block):
        return block[:, :, :HEAD_WIDTH].transpose(1, 0, 2).reshape(count, half_d)

    normed_f, norm1_back = jax.vjp(norm_scale, tokens, gains[:, 0])
    normed = normed_f.astype(bf16)
    proj = jnp.dot(normed, mixer_w, preferred_element_type=f32)
    down_w = gather(tie(to_owner(down_weight.astype(bf16)), proj)).reshape(FF // 2, D)
    query = proj[:, :half_qk].astype(bf16)
    key_vecs = proj[:, half_qk : 2 * half_qk].astype(bf16)
    value = proj[:, 2 * half_qk : 2 * half_qk + half_d].astype(bf16)
    conv_in = proj[:, 2 * half_qk + half_d : 2 * half_qk + 2 * half_d].astype(bf16)
    gate = proj[:, 2 * half_qk + 2 * half_d :]
    key_t = key_vecs.T
    lane = jnp.arange(LANES)
    values = jnp.where(lane == HEAD_WIDTH, jnp.ones((), bf16), per_head(value))
    att, den, carry, halo = attend(
        link, tie(query, gate_w), key_t, values, allow, on[:, None], fresh[None, :], conv_in[count - 16 :],
        tables, ring,
    )
    halo = jnp.where(ring_id == 0, jnp.zeros((), bf16), halo[14:])
    extended = jnp.concatenate([halo, conv_in], axis=0).astype(f32)
    taps = lax.dynamic_slice_in_dim(from_owner(gains[:, 2:5].T), core * half_d, half_d, axis=1)

    def gating(ext_in, taps_in, gate_in):
        return short_conv(ext_in, taps_in, same) * jax.nn.sigmoid(gate_in)

    gated, gate_back = jax.vjp(gating, extended, taps, gate)
    mix_half = (from_heads(att).astype(f32) + gated).astype(bf16)
    mix_other = swap(mix_half)
    output_half = lax.dynamic_slice_in_dim(output_w, core * half_d, half_d, axis=0)
    output_other = lax.dynamic_slice_in_dim(output_w, (1 - core) * half_d, half_d, axis=0)
    branch = dot_nn(mix_half, output_half) + dot_nn(mix_other, output_other)
    middle = tokens + branch
    normed2_f, norm2_back = jax.vjp(norm_scale, middle, gains[:, 1])
    normed2 = normed2_f.astype(bf16)
    gate_in, up_in = dot_nn(normed2, gate_w), dot_nn(normed2, up_w)

    def swiglu(gate_part, up_part):
        return jax.nn.silu(gate_part) * up_part

    inner_f, inner_back = jax.vjp(swiglu, gate_in, up_in)
    inner = inner_f.astype(bf16)
    feed_part = jnp.dot(inner, down_w, preferred_element_type=f32)

    def own_rows(block):
        return lax.dynamic_slice_in_dim(block, core * local_rows, local_rows, axis=0)

    def other_rows(block):
        return lax.dynamic_slice_in_dim(block, (1 - core) * local_rows, local_rows, axis=0)

    def by_owner(grad, rows):
        blocks = grad.reshape(ring, groups, rows, grad.shape[-1])
        return jnp.pad(blocks, ((0, 0), (0, 0), (0, -rows % 16), (0, 0)))

    def inner_dot(left_mat, right_mat):
        return dot_tn(left_mat, right_mat).astype(bf16)

    orders = both_orders(ring, groups)

    def column_parts(left_mat, right_mat, rows):
        cut = right_mat.shape[1] // 2
        return [by_owner(inner_dot(left_mat, part), rows) for part in (right_mat[:, :cut], right_mat[:, cut:])]

    down_chain = Halving(column_parts(inner, upstream, f_rows), orders)
    down_chain.step()
    upstream_after = upstream
    for one in down_chain.step():
        upstream_after = tie(upstream_after, one)
    inner_grad = dot_nt(upstream_after, down_w).astype(bf16)
    gate_part_grad, up_part_grad = [g.astype(bf16) for g in inner_back(inner_grad.astype(f32))]
    updown_parts = [by_owner(inner_dot(normed2, g), 2 * d_rows) for g in (gate_part_grad, up_part_grad)]
    updown_chain = Halving(updown_parts, orders)
    updown_sent = updown_chain.step()
    for one in updown_sent + down_chain.step(updown_sent[1]):
        gate_part_grad = tie(gate_part_grad, one)
    normed2_part = (dot_nt(gate_part_grad, gate_w) + dot_nt(up_part_grad, up_w)).astype(bf16)
    normed2_grad = normed2_part.astype(f32) + swap(normed2_part).astype(f32)
    middle_part, gain2_grad = norm2_back(normed2_grad)
    middle_grad = upstream.astype(f32) + middle_part
    branch_grad = middle_grad.astype(bf16)
    output_part = inner_dot(mix_half, branch_grad).reshape(ring // 2, 2, groups * d_rows, D)
    output_keep = lax.dynamic_index_in_dim(output_part, core, axis=1, keepdims=False)
    output_send = lax.dynamic_index_in_dim(output_part, 1 - core, axis=1, keepdims=False)
    output_part = in_order(core, output_keep, swap(output_send)).reshape(ring, groups, d_rows, D)
    output_part = jnp.concatenate([output_part[..., :half_d], output_part[..., half_d:]], axis=2)
    output_part = by_owner(output_part.reshape(D, half_d), 2 * d_rows)
    mix_grad = dot_nt(branch_grad, output_half).astype(bf16)
    ext_grad, taps_grad, gate_grad = gate_back(mix_grad.astype(f32))
    head_grad = mix_grad
    for got in updown_chain.got:
        head_grad = tie(head_grad, got)
    query_g, key_g, value_g, after = attend_back(
        link, query, key_vecs, query.T, key_t, values, per_head(head_grad), att, den, carry, allow, on[:, None],
        on[None, :], fresh[:, None], ext_grad[:8], tables, ring, [],
    )
    sent = updown_chain.step(key_g) + down_chain.step(key_g)
    after = jnp.where(ring_id == ring - 1, 0.0, after[:2])
    conv_grad = ext_grad[2:] + jnp.pad(after, ((count - 2, 0), (0, 0)))
    proj_grad = jnp.concatenate(
        [
            query_g.astype(bf16), key_g.astype(bf16), from_heads(value_g),
            conv_grad.astype(bf16), gate_grad.astype(bf16),
        ],
        axis=1,
    )
    for one in sent:
        proj_grad = tie(proj_grad, one)
    mixer_part = by_owner(inner_dot(normed, proj_grad), 2 * d_rows)
    normed_part = dot_nt(proj_grad, mixer_w)
    normed_grad = own_rows(normed_part) + swap(other_rows(normed_part))
    tokens_own = own_rows(tokens)
    ignored, norm1_back_own = jax.vjp(norm_scale, tokens_own, gains[:, 0])
    input_part, gain1_grad = norm1_back_own(normed_grad)
    input_grad = from_owner(own_rows(middle_grad) + input_part)

    keys = sorted(updown_chain.place, key=updown_chain.place.get)

    def by_bits(partial):
        return partial.reshape((2,) * len(keys) + partial.shape[2:])

    arrays, specs, widths = [], [], []

    def add_chains(array, columns, chain_keys, chain_orders, ranks):
        at = 0
        for number, width in enumerate(columns):
            specs.append((len(arrays), at, width, chain_keys, chain_orders[number % len(chain_orders)], ranks[number]))
            at += width
        arrays.append(array)
        widths.append(len(columns))

    for number, (left, left_keys, order) in enumerate(updown_chain.rest()):
        add_chains(left, [FF // 4, FF // 4], left_keys, [order], [number / 2, 1 + number / 2])
    add_chains(by_bits(mixer_part), [512] * 5 + [384], keys, orders, [0.0, 0.0, 1.0, 1.0, 2.0, 2.0])
    add_chains(by_bits(output_part), [512, 384], keys, orders, [3.0, 3.0])
    summed = reduce_rest(arrays, specs)
    wholes = []
    for number in widths:
        wholes.append(jnp.concatenate(summed[:number], axis=1))
        summed = summed[number:]
    updown_sum = jnp.concatenate(wholes[:2], axis=1)
    down_sum = from_owner(down_chain.result()[:f_rows])
    mixer_sum = wholes[2]
    output_sum = from_owner(
        wholes[3][: 2 * d_rows].reshape(2, d_rows, half_d).transpose(1, 0, 2).reshape(d_rows, D)
    )

    feed = own_rows(feed_part) + swap(tie(other_rows(feed_part), key_g))
    middle_own = own_rows(middle)
    layer = from_owner((middle_own + feed).astype(bf16))
    branch_own = own_rows(branch)
    stats = jnp.stack([jnp.sum(middle_own * middle_own), jnp.sum(branch_own * branch_own), jnp.sum(feed * feed)])

    taps_wide = lax.dynamic_update_slice(jnp.zeros((3, D), f32), taps_grad, (0, core * half_d))
    gain_grad = jnp.concatenate([from_owner(jnp.stack([gain1_grad, 0.5 * gain2_grad])), taps_wide], axis=0)

    square = functools.reduce(jnp.add, [jnp.sum(g * g) for g in (mixer_sum, updown_sum, down_sum, output_sum)])
    spots = jnp.arange(D)[None, :]
    numbers = functools.reduce(
        jnp.add, [jnp.where(spots == i, n, 0.0) for i, n in enumerate((square, stats[0], stats[1], stats[2]))]
    )
    sums = sum_everywhere(jnp.concatenate([gain_grad, numbers, jnp.zeros((2, D), f32)], axis=0), ring, groups)
    gain_total = sums[:5]
    total_sq = sums[5, 0] + jnp.sum(gain_total * gain_total)
    stat_sum = sums[5, 1:4]
    place = (ring_id * 2 + core) * groups + lax.axis_index("fsdp")
    gain_sum = lax.dynamic_index_in_dim(
        gain_total.reshape(5, 2 * ring * groups, d_rows), place, axis=1, keepdims=False
    ).T

    def own_whole(summed):
        blocks = summed[: 2 * d_rows].reshape(2, d_rows, summed.shape[-1])
        keep_rows = lax.dynamic_index_in_dim(blocks, core, axis=0, keepdims=False)
        send_rows = lax.dynamic_index_in_dim(blocks, 1 - core, axis=0, keepdims=False)
        return in_order(core, keep_rows, swap(send_rows))

    mixer_own = own_whole(mixer_sum)
    pieces, at = [], 0
    for width in (half_qk, half_qk, half_d, half_d, half_d):
        pieces += [mixer_own[0, :, at : at + width], mixer_own[1, :, at : at + width]]
        at += width
    mixer_own = jnp.concatenate(pieces, axis=1)
    updown_own = own_whole(updown_sum).reshape(2, d_rows, 2, ring, pair_ff)
    updown_own = updown_own.transpose(1, 2, 3, 0, 4).reshape(d_rows, 2 * FF)
    grad_list = (mixer_own, output_sum, updown_own, down_sum, gain_sum)
    grad_norm = jnp.sqrt(total_sq)
    factor = jnp.minimum(1.0, clip_level / grad_norm)
    masters = (mixer_weight, output_weight, updown_weight, down_weight, gain_weight)
    firsts = (mixer_first, output_first, updown_first, down_first, gain_first)
    seconds = (mixer_second, output_second, updown_second, down_second, gain_second)
    nexts, moms, varis = ([], [], [])
    for index in range(5):
        rate = rate_gain if index == 4 else rate_matrix
        decay = 0.0 if index == 4 else decay_rate
        new_w, new_m, new_v = adam_step(
            masters[index], firsts[index], seconds[index], grad_list[index] * factor, rate, decay
        )
        nexts.append(new_w)
        moms.append(new_m)
        varis.append(new_v)
    layer_rms = jnp.sqrt(stat_sum / (count * ring * groups * D))
    return (layer[None], input_grad[None], *nexts, *moms, *varis, grad_norm, layer_rms)


def solution(mesh):
    shards, groups = mesh.shape["seq"], mesh.shape["fsdp"]
    split = Mesh(mesh.devices.reshape(shards // 2, 2, groups), ("ring", "core", "fsdp"))
    tokens = P("fsdp", ("ring", "core"), None)
    rows = P(("ring", "core", "fsdp"), None)
    pack = P("fsdp", None)
    return jax.shard_map(
        per_device,
        mesh=split,
        in_specs=(tokens,) * 2 + (rows,) * 15 + (pack,) * 3,
        out_specs=(tokens,) * 2 + (rows,) * 15 + (P(), P()),
        check_vma=False,
    )
```

```python
import functools

import jax
import jax.numpy as jnp
import numpy as np
from jax import lax
from jax.experimental import pallas as pl
from jax.experimental.layout import Layout, with_layout_constraint
from jax.experimental.pallas import tpu as pltpu
from jax.sharding import Mesh
from jax.sharding import PartitionSpec as P

D = 1792
HEADS = 16
FEAT = 16
FF = 4096
STEP = 10
HALF_HEADS = HEADS // 2
HEAD_WIDTH = D // HEADS
PHI = 160
LANES = 128
TILE = 256

norm_eps = 1e-06
beta_one = 0.9
beta_two = 0.95
adam_eps = 1e-08
rate_matrix = 0.05
rate_gain = 1.5
decay_rate = 0.1
clip_level = 1.0

bf16 = jnp.bfloat16
f32 = jnp.float32
VMEM_LIMIT = 48 * 1024 * 1024
GATHER_PACE = (-2.0, -1.2, 0.0, 1.1)
REDUCE_PACE = (0.0, 1.5, 2.6, 3.7, 4.8)


def feature_tables():
    first = np.zeros((FEAT, PHI), np.float32)
    second = np.zeros((FEAT, PHI), np.float32)
    bias = np.zeros((2, PHI), np.float32)
    scale = np.zeros((PHI,), np.float32)
    bias[:, 0] = 1.0
    scale[0] = 1.0
    at = 1
    for a in range(FEAT):
        first[a, at] = 1.0
        bias[1, at] = 1.0
        scale[at] = FEAT**-0.5
        at += 1
    for a in range(FEAT):
        for b in range(a, FEAT):
            first[a, at] = 1.0
            second[b, at] = 1.0
            scale[at] = (1.0 if a == b else 2.0) / (2.0 * FEAT)
            at += 1
    return first, second, bias, scale


def dot_nn(a, b):
    return lax.dot_general(a, b, (((1,), (0,)), ((), ())), preferred_element_type=f32)


def dot_tn(a, b):
    return lax.dot_general(a, b, (((0,), (0,)), ((), ())), preferred_element_type=f32)


def dot_nt(a, b):
    return lax.dot_general(a, b, (((1,), (1,)), ((), ())), preferred_element_type=f32)


def bits_of(size):
    return size.bit_length() - 1


def other(axis, bit):
    me = lax.axis_index(axis)
    return {axis: me + (1 - 2 * ((me // 2**bit) % 2)) * 2**bit}


def greet(partners):
    barrier = pltpu.get_barrier_semaphore()
    for partner in partners:
        pl.semaphore_signal(barrier, inc=1, device_id=partner, device_id_type=pl.DeviceIdType.MESH)
    pl.semaphore_wait(barrier, len(partners))


def gather_kernel(ring, groups, parts, orders, count, shared, *refs):
    in_refs, out_refs = refs[:count], refs[count : 2 * count]
    send_sem, recv_sem, own_sem = refs[2 * count :]
    ring_bits, group_bits = bits_of(ring), bits_of(groups)
    every = [("ring", b) for b in reversed(range(ring_bits))] + [("fsdp", b) for b in reversed(range(group_bits))]
    partners = {key: other(*key) for key in every}
    core_partner = other("core", 0)
    greet(list(partners.values()) + [core_partner])
    core = lax.axis_index("core")
    bit = {(axis, b): (lax.axis_index(axis) // 2**b) % 2 for axis, b in every}

    def view(ref, have, columns):
        spots = [slice(None) if key in have else pl.ds(bit[key], 1) for key in every]
        spots.insert(ring_bits, slice(None))
        return ref.at[tuple(spots) + (slice(None), columns)]

    def placed(part):
        index, at, width = parts[part]
        if index not in shared:
            return pl.ds(at, width)
        return pl.ds(pl.multiple_of(core * in_refs[index].shape[-1] + at, LANES), width)

    steps = len(every)
    events = []
    for part in range(len(parts)):
        for step in range(steps):
            late = GATHER_PACE[min(max(step + 4 - steps, 0), 3)]
            events.append((part // 2 + late, part, step))
    copies, owns = {}, []
    for index in range(count):
        everything = slice(None)
        if index in shared:
            columns = in_refs[index].shape[-1]
            everything = pl.ds(pl.multiple_of(core * columns, LANES), columns)
        owns.append(
            pltpu.make_async_copy(in_refs[index], view(out_refs[index], (), everything), own_sem.at[index])
        )
    owned = False
    for _, part, step in sorted(events):
        if step and not owned:
            owned = True
            for own in owns:
                own.start()
            for own in owns:
                own.wait()
        order = orders[part % len(orders)]
        if step:
            copies[part, step - 1].wait_recv()
        index, at, width = parts[part]
        ndim = in_refs[index].ndim
        here = view(out_refs[index], order[:step], placed(part))
        source = in_refs[index].at[(slice(None),) * (ndim - 1) + (pl.ds(at, width),)] if step == 0 else here
        copies[part, step] = pltpu.make_async_remote_copy(
            src_ref=source,
            dst_ref=here,
            send_sem=send_sem.at[part, step],
            recv_sem=recv_sem.at[part, step],
            device_id=partners[order[step]],
            device_id_type=pl.DeviceIdType.MESH,
        )
        copies[part, step].start()
    for part in range(len(parts)):
        copies[part, steps - 1].wait_recv()
        if parts[part][0] in shared:
            here = view(out_refs[parts[part][0]], every, placed(part))
            copies[part, steps] = pltpu.make_async_remote_copy(
                src_ref=here,
                dst_ref=here,
                send_sem=send_sem.at[part, steps],
                recv_sem=recv_sem.at[part, steps],
                device_id=core_partner,
                device_id_type=pl.DeviceIdType.MESH,
            )
            copies[part, steps].start()
    for part in range(len(parts)):
        if parts[part][0] in shared:
            copies[part, steps].wait_recv()
    for copy in copies.values():
        copy.wait_send()


def gather_rows(blocks, cuts, shared, ring, groups):
    ring_bits, group_bits = bits_of(ring), bits_of(groups)
    near, far = [("ring", 0)], [("ring", b) for b in reversed(range(1, ring_bits))]
    group = [("fsdp", b) for b in reversed(range(group_bits))]
    orders = (far + near + group, far + group + near)
    parts = []
    for index, widths in enumerate(cuts):
        at = 0
        for width in widths:
            parts.append((index, at, width))
            at += width
    steps = ring_bits + group_bits
    ins, shapes, size = [], [], 0
    for block in blocks:
        cores, rows, columns = block.shape
        ins.append(block.reshape((1,) * ring_bits + (cores,) + (1,) * group_bits + (rows, columns)))
        width = 2 * columns if len(ins) - 1 in shared else columns
        shape = (2,) * ring_bits + (cores,) + (2,) * group_bits + (rows, width)
        shapes.append(jax.ShapeDtypeStruct(shape, block.dtype))
        size += 2 * block.size * ring * groups
    outs = pl.pallas_call(
        functools.partial(gather_kernel, ring, groups, parts, orders, len(blocks), shared),
        in_specs=[pl.BlockSpec(memory_space=pl.ANY)] * len(blocks),
        out_specs=[pl.BlockSpec(memory_space=pl.ANY)] * len(blocks),
        out_shape=shapes,
        scratch_shapes=[
            pltpu.SemaphoreType.DMA((len(parts), steps + 1)),
            pltpu.SemaphoreType.DMA((len(parts), steps + 1)),
            pltpu.SemaphoreType.DMA((len(blocks),)),
        ],
        compiler_params=pltpu.CompilerParams(collective_id=0, has_side_effects=True),
        cost_estimate=pl.CostEstimate(flops=0, bytes_accessed=20 * size, transcendentals=0),
        name="gather_rows",
    )(*ins)
    return [o.reshape((2 * ring * groups if b.shape[0] == 2 else ring * groups) * b.shape[1], o.shape[-1])
            for o, b in zip(outs, blocks)]


def reduce_kernel(chains, partners, pairs, *refs):
    refs = list(refs)

    def take(number):
        taken = refs[:number]
        del refs[:number]
        return taken

    in_refs, out_refs = take(pairs), take(len(chains))
    own_refs = take(len(chains))
    recv_refs = [take(len(chain[4])) for chain in chains]
    send_refs = [take(len(chain[4]) - 1) for chain in chains]
    send_sem, recv_sem, own_sem = take(3)
    greet([other(*key) for key in partners])
    mine = {(axis, b): (lax.axis_index(axis) // 2**b) % 2 for axis, b in partners}
    copies = {}

    def start(c, step, source):
        copies[c, step] = pltpu.make_async_remote_copy(
            src_ref=source,
            dst_ref=recv_refs[c][step],
            send_sem=send_sem.at[c, step],
            recv_sem=recv_sem.at[c, step],
            device_id=other(*chains[c][4][step]),
            device_id_type=pl.DeviceIdType.MESH,
        )
        copies[c, step].start()

    def first_half(c, side):
        source, at, width, keys, order, rank = chains[c]
        spots = tuple(side if key == order[0] else slice(None) for key in keys)
        return in_refs[source].at[spots + (slice(None), pl.ds(at, width))]

    def add_up(c, step, target):
        keys, order = chains[c][3], chains[c][4]
        left = [key for key in keys if key not in order[: step + 1]]
        rows = target.shape[-2]
        tile = 16 if rows % 16 == 0 else rows
        for spot in np.ndindex(*(2,) * len(left)):
            spot = tuple(int(i) for i in spot)
            free = dict(zip(left, spot))

            def where(key):
                if key in free:
                    return free[key]
                return 1 - mine[key] if step < len(order) and key == order[step] else mine[key]

            def body(i, carry):
                at = pl.ds(pl.multiple_of(i * tile, tile), tile)
                total = None
                for t in range(step + 1):
                    ref = own_refs[c] if t == 0 else recv_refs[c][t - 1]
                    index = tuple(where(key) for key in keys if key not in order[: max(t, 1)])
                    term = ref[index + (at, slice(None))].astype(f32)
                    total = term if total is None else total + term
                target[spot + (at, slice(None))] = total.astype(target.dtype)
                return carry

            lax.fori_loop(0, rows // tile, body, 0)

    owns = []
    for c in range(len(chains)):
        own = pltpu.make_async_copy(first_half(c, mine[chains[c][4][0]]), own_refs[c], own_sem.at[c])
        own.start()
        owns.append(own)
    events = []
    for c, chain in enumerate(chains):
        for step in range(len(chain[4]) + 1):
            events.append((chain[5] + REDUCE_PACE[min(step, 4)], c, step))
    for _, c, step in sorted(events):
        order = chains[c][4]
        if step == 0:
            start(c, 0, first_half(c, 1 - mine[order[0]]))
            continue
        if step == 1:
            owns[c].wait()
        copies[c, step - 1].wait_recv()
        if step < len(order):
            add_up(c, step, send_refs[c][step - 1])
            start(c, step, send_refs[c][step - 1])
        else:
            add_up(c, step, out_refs[c])
    for copy in copies.values():
        copy.wait_send()


def reduce_rest(arrays, specs):
    outs, owns, recvs, sends = [], [], [], []
    steps = 0
    for source, at, width, keys, order, rank in specs:
        rows = arrays[source].shape[-2]
        steps = max(steps, len(order))
        outs.append(jax.ShapeDtypeStruct((rows, width), f32))
        shapes = [(2,) * (len(keys) - step - 1) + (rows, width) for step in range(len(order))]
        owns.append(pltpu.VMEM(shapes[0], bf16))
        recvs += [pltpu.VMEM(shape, bf16) for shape in shapes]
        sends += [pltpu.VMEM(shape, bf16) for shape in shapes[1:]]
    partners = sorted({key for spec in specs for key in spec[4]})
    sems = (len(specs), steps)
    return pl.pallas_call(
        functools.partial(reduce_kernel, specs, partners, len(arrays)),
        in_specs=[pl.BlockSpec(memory_space=pl.ANY)] * len(arrays),
        out_specs=[pl.BlockSpec(memory_space=pltpu.VMEM)] * len(specs),
        out_shape=outs,
        scratch_shapes=owns
        + recvs
        + sends
        + [
            pltpu.SemaphoreType.DMA(sems),
            pltpu.SemaphoreType.DMA(sems),
            pltpu.SemaphoreType.DMA((len(specs),)),
        ],
        compiler_params=pltpu.CompilerParams(
            collective_id=2, has_side_effects=True, vmem_limit_bytes=58 * 1024 * 1024
        ),
        name="reduce_rest",
    )(*arrays)


def sum_kernel(partners, in_ref, out_ref, held, got, send_sem, recv_sem):
    partners = [other(*key) for key in partners]
    greet(partners)
    held[0] = in_ref[...]
    for step, partner in enumerate(partners):
        copy = pltpu.make_async_remote_copy(
            src_ref=held.at[step],
            dst_ref=got.at[step],
            send_sem=send_sem.at[step],
            recv_sem=recv_sem.at[step],
            device_id=partner,
            device_id_type=pl.DeviceIdType.MESH,
        )
        copy.start()
        copy.wait()
        total = held[step] + got[step]
        if step + 1 < len(partners):
            held[step + 1] = total
        else:
            out_ref[...] = total


def sum_everywhere(block, ring, groups):
    partners = [("core", 0)] + [("ring", b) for b in range(bits_of(ring))] + [("fsdp", b) for b in range(bits_of(groups))]
    steps = len(partners)
    return pl.pallas_call(
        functools.partial(sum_kernel, partners),
        in_specs=[pl.BlockSpec(memory_space=pltpu.VMEM)],
        out_specs=pl.BlockSpec(memory_space=pltpu.VMEM),
        out_shape=jax.ShapeDtypeStruct(block.shape, f32),
        scratch_shapes=[
            pltpu.VMEM((steps,) + block.shape, f32),
            pltpu.VMEM((steps,) + block.shape, f32),
            pltpu.SemaphoreType.DMA((steps,)),
            pltpu.SemaphoreType.DMA((steps,)),
        ],
        compiler_params=pltpu.CompilerParams(collective_id=1, has_side_effects=True),
        name="sum_everywhere",
    )(block)


def exchange(source, target, send_sem, recv_sem):
    ring = source.shape[0]
    me = lax.axis_index("ring")
    copies = []
    for away in range(1, ring):
        peer = (me + away) % ring
        copy = pltpu.make_async_remote_copy(
            src_ref=source.at[peer],
            dst_ref=target.at[me],
            send_sem=send_sem.at[away],
            recv_sem=recv_sem.at[away],
            device_id={"ring": peer},
            device_id_type=pl.DeviceIdType.MESH,
        )
        copy.start()
        copies.append(copy)
    target[me] = source[me]
    return copies


def pass_along(source, target, away, send_sem, recv_sem):
    ring = lax.axis_size("ring")
    copy = pltpu.make_async_remote_copy(
        src_ref=source,
        dst_ref=target,
        send_sem=send_sem,
        recv_sem=recv_sem,
        device_id={"ring": (lax.axis_index("ring") + ring + away) % ring},
        device_id_type=pl.DeviceIdType.MESH,
    )
    copy.start()
    return copy


def arrive(copies):
    for copy in copies:
        copy.wait_recv()


def leave(copies):
    for copy in copies:
        copy.wait_send()


def greet_ring(ring):
    me = lax.axis_index("ring")
    greet([{"ring": (me + away) % ring} for away in range(1, ring)])


def put_state(buffer, head, state):
    ring, piece = buffer.shape[0], buffer.shape[1]
    share = ring // HALF_HEADS
    for part in range(share):
        buffer[head * share + part] = state[part * piece : (part + 1) * piece].astype(bf16)


def get_state(buffer, head):
    share = buffer.shape[0] // HALF_HEADS
    if share == 1:
        return buffer[head]
    return jnp.concatenate([buffer[head * share + part] for part in range(share)], axis=0)


def linked(states, link_ref, target, backward):
    ring = states.shape[0]
    for d in range(ring):
        total = jnp.zeros(states.shape[1:], f32)
        for e in range(d + 1, ring) if backward else range(d):
            weight = link_ref[e, d] if backward else link_ref[d, e]
            total = total + weight * states[e].astype(f32)
        target[d] = total.astype(bf16)


def attend_kernel(
    ring, link_ref, q_ref, kt_ref, v_ref, allow_ref, on_ref, fresh_ref, first_ref, second_ref, row_ref,
    first_t_ref, second_t_ref, col_ref, edge_ref, att_ref, den_ref, carry_ref, halo_ref,
    num_ref, one_ref, two_ref, three_ref, send_sem, recv_sem,
):
    count = q_ref.shape[0]
    lane = lax.broadcasted_iota(jnp.int32, (1, LANES), 1)
    rows, cols = row_ref[...], col_ref[...]
    greet_ring(ring)
    halo = [pass_along(edge_ref, halo_ref, 1, send_sem.at[0, 0], recv_sem.at[0, 0])]

    def local_state(head, none):
        kt = kt_ref[pl.ds(pl.multiple_of(head * FEAT, FEAT), FEAT), :]
        one = dot_nn(first_t_ref[...], kt) + cols[:, 0:1]
        two = dot_nn(second_t_ref[...], kt) + cols[:, 1:2]
        phi = (one * two * cols[:, 2:3] * fresh_ref[...]).astype(bf16)
        put_state(one_ref, head, dot_nn(phi, v_ref[head]))
        return none

    lax.fori_loop(0, HALF_HEADS, local_state, 0)

    def within(head, none):
        mine = (lane // FEAT == head).astype(bf16)
        for i in range(count // TILE):
            at = slice(i * TILE, (i + 1) * TILE)
            q = q_ref[at, :] * mine
            num = jnp.zeros((TILE, LANES), f32)
            for j in range(i + 1):
                to = slice(j * TILE, (j + 1) * TILE)
                dots = dot_nn(q, kt_ref[:, to]) * FEAT**-0.5 + 1.0
                score = (0.5 * dots * dots + 0.5) * allow_ref[at, to].astype(f32)
                num = num + dot_nn(score.astype(bf16), v_ref[head, to, :])
            num_ref[head, at, :] = num
        return none

    copies = exchange(one_ref, two_ref, send_sem.at[0], recv_sem.at[0])
    lax.fori_loop(0, HALF_HEADS // 2, within, 0)
    arrive(copies)
    linked(two_ref, link_ref, three_ref, False)
    back = exchange(three_ref, carry_ref, send_sem.at[1], recv_sem.at[1])
    lax.fori_loop(HALF_HEADS // 2, HALF_HEADS, within, 0)
    arrive(back)
    den_ref[...] = jnp.zeros_like(den_ref)

    def finish(head, none):
        mine = (lane // FEAT == head).astype(bf16)
        carry = get_state(carry_ref, head)
        for i in range(count // TILE):
            at = slice(i * TILE, (i + 1) * TILE)
            q = q_ref[at, :] * mine
            phi = (dot_nn(q, first_ref[...]) + rows[0:1]) * (dot_nn(q, second_ref[...]) + rows[1:2])
            num = num_ref[head, at, :] + dot_nn(phi.astype(bf16), carry) * on_ref[at, :]
            den = num[:, HEAD_WIDTH : HEAD_WIDTH + 1] + 1.0
            att_ref[head, at, :] = (num / den).astype(bf16)
            den_ref[at, :] += jnp.where(lane == head, den, 0.0)
        return none

    lax.fori_loop(0, HALF_HEADS, finish, 0)
    arrive(halo)
    leave(copies + back + halo)


def attend_back_kernel(
    ring, after, link_ref, q_ref, k_ref, qt_ref, kt_ref, v_ref, up_ref, att_ref, den_ref, carry_ref, allow_ref,
    on_ref, on_row_ref, fresh_ref, first_ref, second_ref, row_ref, first_t_ref, second_t_ref, col_ref, edge_ref, *refs,
):
    dq_ref, dk_ref, dv_ref, halo_ref = refs[after : after + 4]
    a_ref, dvs_ref, one_ref, two_ref, three_ref, later_ref, send_sem, recv_sem = refs[after + 4 :]
    count = q_ref.shape[0]
    tiles = count // TILE
    lane = lax.broadcasted_iota(jnp.int32, (1, LANES), 1)
    rows, cols = row_ref[...], col_ref[...]
    first, second = first_ref[...], second_ref[...]
    greet_ring(ring)
    halo = [pass_along(edge_ref, halo_ref, -1, send_sem.at[0, 0], recv_sem.at[0, 0])]
    dq_ref[...] = jnp.zeros_like(dq_ref)
    dk_ref[...] = jnp.zeros_like(dk_ref)

    def query_state(head, none):
        den = jnp.sum(jnp.where(lane == head, den_ref[...], 0.0), axis=1, keepdims=True)
        g = jnp.where(lane < HEAD_WIDTH, up_ref[head].astype(f32) / den, 0.0)
        back = jnp.sum(g * att_ref[head].astype(f32), axis=1, keepdims=True)
        a = jnp.where(lane == HEAD_WIDTH, -back, g).astype(bf16)
        a_ref[head] = a
        qt = qt_ref[pl.ds(pl.multiple_of(head * FEAT, FEAT), FEAT), :]
        one = dot_nn(first_t_ref[...], qt) + cols[:, 0:1]
        two = dot_nn(second_t_ref[...], qt) + cols[:, 1:2]
        phi = (one * two * on_row_ref[...]).astype(bf16)
        put_state(one_ref, head, dot_nn(phi, a))
        return none

    lax.fori_loop(0, HALF_HEADS, query_state, 0)

    def through(vec, d_phi):
        one = dot_nn(vec, first) + rows[0:1]
        two = dot_nn(vec, second) + rows[1:2]
        grad = dot_nt((d_phi * two).astype(bf16), first) + dot_nt((d_phi * one).astype(bf16), second)
        return grad, one * two

    def within(head, none):
        here = lane // FEAT == head
        mine = here.astype(bf16)
        carry = get_state(carry_ref, head)
        q = [q_ref[i * TILE : (i + 1) * TILE, :] * mine for i in range(tiles)]
        k = [k_ref[i * TILE : (i + 1) * TILE, :] * mine for i in range(tiles)]
        dk, dv = [None] * tiles, [None] * tiles
        for i in reversed(range(tiles)):
            at = slice(i * TILE, (i + 1) * TILE)
            a = a_ref[head, at, :]
            dq = through(q[i], dot_nt(a, carry) * on_ref[at, :])[0]
            for j in range(i + 1):
                to = slice(j * TILE, (j + 1) * TILE)
                allow = allow_ref[at, to].astype(f32)
                dots = dot_nn(q[i], kt_ref[:, to]) * FEAT**-0.5 + 1.0
                score = ((0.5 * dots * dots + 0.5) * allow).astype(bf16)
                d_dots = dot_nt(a, v_ref[head, to, :]) * dots * allow * FEAT**-0.5
                d_dots = d_dots.astype(bf16)
                dq = dq + dot_nn(d_dots, k[j])
                dk_more, dv_more = dot_tn(d_dots, q[i]), dot_tn(score, a)
                dk[j] = dk_more if dk[j] is None else dk[j] + dk_more
                dv[j] = dv_more if dv[j] is None else dv[j] + dv_more
            dq_ref[at, :] += jnp.where(here, dq, 0.0)
        for j in range(tiles):
            to = slice(j * TILE, (j + 1) * TILE)
            dk_ref[to, :] += jnp.where(here, dk[j], 0.0)
            dvs_ref[head, to, :] = dv[j]
        return none

    copies = exchange(one_ref, two_ref, send_sem.at[0], recv_sem.at[0])
    lax.fori_loop(0, HALF_HEADS // 2, within, 0)
    arrive(copies)
    linked(two_ref, link_ref, three_ref, True)
    back = exchange(three_ref, later_ref, send_sem.at[1], recv_sem.at[1])
    lax.fori_loop(HALF_HEADS // 2, HALF_HEADS, within, 0)
    arrive(back)

    def finish(head, none):
        here = lane // FEAT == head
        mine = here.astype(bf16)
        later = get_state(later_ref, head)
        for i in range(tiles):
            at = slice(i * TILE, (i + 1) * TILE)
            d_phi = dot_nt(v_ref[head, at, :], later) * rows[2:3] * fresh_ref[at, :]
            grad, phi = through(k_ref[at, :] * mine, d_phi)
            dk_ref[at, :] += jnp.where(here, grad, 0.0)
            phi = (phi * rows[2:3] * fresh_ref[at, :]).astype(bf16)
            dv_ref[head, at, :] = (dvs_ref[head, at, :] + dot_nn(phi, later)).astype(bf16)
        return none

    lax.fori_loop(0, HALF_HEADS, finish, 0)
    arrive(halo)
    leave(copies + back + halo)


def state_blocks(ring):
    return (ring, HALF_HEADS * PHI // ring, LANES)


def attend(link, q, kt, values, allow, on_col, fresh_row, edge, tables, ring):
    count = q.shape[0]
    vmem, smem = pl.BlockSpec(memory_space=pltpu.VMEM), pl.BlockSpec(memory_space=pltpu.SMEM)
    blocks = state_blocks(ring)
    return pl.pallas_call(
        functools.partial(attend_kernel, ring),
        in_specs=[smem] + [vmem] * 13,
        out_specs=[vmem] * 4,
        out_shape=[
            jax.ShapeDtypeStruct((HALF_HEADS, count, LANES), bf16),
            jax.ShapeDtypeStruct((count, LANES), f32),
            jax.ShapeDtypeStruct(blocks, bf16),
            jax.ShapeDtypeStruct(edge.shape, edge.dtype),
        ],
        scratch_shapes=[
            pltpu.VMEM((HALF_HEADS, count, LANES), f32),
            pltpu.VMEM(blocks, bf16),
            pltpu.VMEM(blocks, bf16),
            pltpu.VMEM(blocks, bf16),
            pltpu.SemaphoreType.DMA((2, ring)),
            pltpu.SemaphoreType.DMA((2, ring)),
        ],
        compiler_params=pltpu.CompilerParams(collective_id=3, has_side_effects=True, vmem_limit_bytes=VMEM_LIMIT),
        name="attend",
    )(link, q, kt, values, allow, on_col, fresh_row, tables["first"], tables["second"], tables["rows"],
      tables["first_t"], tables["second_t"], tables["cols"], edge)


def attend_back(link, q, k, qt, kt, values, upstream, att, den, carry, allow, on_col, on_row, fresh_col, edge, tables, ring, after):
    count = q.shape[0]
    vmem, smem = pl.BlockSpec(memory_space=pltpu.VMEM), pl.BlockSpec(memory_space=pltpu.SMEM)
    blocks = state_blocks(ring)
    return pl.pallas_call(
        functools.partial(attend_back_kernel, ring, len(after)),
        in_specs=[smem] + [vmem] * 20 + [pl.BlockSpec(memory_space=pl.ANY)] * len(after),
        out_specs=[vmem] * 4,
        out_shape=[
            jax.ShapeDtypeStruct((count, LANES), f32),
            jax.ShapeDtypeStruct((count, LANES), f32),
            jax.ShapeDtypeStruct((HALF_HEADS, count, LANES), bf16),
            jax.ShapeDtypeStruct(edge.shape, edge.dtype),
        ],
        scratch_shapes=[
            pltpu.VMEM((HALF_HEADS, count, LANES), bf16),
            pltpu.VMEM((HALF_HEADS, count, LANES), f32),
            pltpu.VMEM(blocks, bf16),
            pltpu.VMEM(blocks, bf16),
            pltpu.VMEM(blocks, bf16),
            pltpu.VMEM(blocks, bf16),
            pltpu.SemaphoreType.DMA((2, ring)),
            pltpu.SemaphoreType.DMA((2, ring)),
        ],
        compiler_params=pltpu.CompilerParams(collective_id=4, has_side_effects=True, vmem_limit_bytes=VMEM_LIMIT),
        name="attend_back",
    )(link, q, k, qt, kt, values, upstream, att, den, carry, allow, on_col, on_row, fresh_col,
      tables["first"], tables["second"], tables["rows"], tables["first_t"], tables["second_t"], tables["cols"], edge,
      *after)


def make_tables():
    first, second, bias, scale = feature_tables()
    rows = np.concatenate([bias, scale[None]], axis=0)
    return {
        "first": jnp.asarray(np.tile(first, (HALF_HEADS, 1)), bf16),
        "second": jnp.asarray(np.tile(second, (HALF_HEADS, 1)), bf16),
        "first_t": jnp.asarray(first.T, bf16),
        "second_t": jnp.asarray(second.T, bf16),
        "rows": jnp.asarray(rows, f32),
        "cols": jnp.asarray(rows.T, f32),
    }


def row_major(array):
    return with_layout_constraint(array, Layout(major_to_minor=tuple(range(array.ndim))))


def swap(block):
    return lax.ppermute(block, "core", [(0, 1), (1, 0)])


def in_order(core, mine, theirs):
    return jnp.stack([jnp.where(core == 0, mine, theirs), jnp.where(core == 0, theirs, mine)])


def choose(core, zero, one):
    return jnp.where(core == 0, zero, one)


def tie(block, after):
    if after is None:
        return block
    zero = lax.slice(after, (0,) * after.ndim, (1,) * after.ndim).reshape((1,) * block.ndim) * 0
    return block + zero.astype(block.dtype)


class Halving:
    def __init__(self, parts, orders):
        ring, groups = lax.axis_size("ring"), lax.axis_size("fsdp")
        ring_bits, group_bits = bits_of(ring), bits_of(groups)
        self.place = {("ring", b): ring_bits - 1 - b for b in range(ring_bits)}
        self.place.update({("fsdp", b): ring_bits + group_bits - 1 - b for b in range(group_bits)})
        self.index = {axis: lax.axis_index(axis) for axis in ("ring", "fsdp")}
        shape = (2,) * (ring_bits + group_bits)
        self.parts = [[part.reshape(shape + part.shape[2:])] for part in parts]
        self.orders = orders
        self.at = 0

    def step(self, after=None):
        sent, self.got = [], []
        for which, order in enumerate(self.orders):
            axis, bit = order[self.at]
            dim = self.place[axis, bit]
            mine = (self.index[axis] >> bit) & 1

            def half(term, side):
                return lax.dynamic_slice_in_dim(term, side, 1, axis=dim)

            terms = self.parts[which]
            send = functools.reduce(jnp.add, [half(t, 1 - mine).astype(f32) for t in terms]).astype(bf16)
            send = tie(send, after)
            size = lax.axis_size(axis)
            got = lax.ppermute(send, axis, [(i, i ^ (1 << bit)) for i in range(size)])
            self.parts[which] = [half(t, mine) for t in terms] + [got]
            sent.append(send)
            self.got.append(got)
        self.at += 1
        return sent

    def rest(self):
        found = []
        for terms, order in zip(self.parts, self.orders):
            gone = [self.place[key] for key in order[: self.at]]
            total = functools.reduce(jnp.add, [t.astype(f32) for t in terms]).astype(bf16)
            left = total.reshape([n for dim, n in enumerate(total.shape) if dim not in gone])
            keys = sorted(order[self.at :], key=self.place.get)
            found.append((left, keys, order[self.at :]))
        return found


    def result(self):
        while self.at < len(self.orders[0]):
            self.step()
        totals = []
        for terms in self.parts:
            total = functools.reduce(jnp.add, [t.astype(f32) for t in terms])
            totals.append(total.reshape(total.shape[-2:]))
        return jnp.concatenate(totals, axis=-1)


def both_orders(ring, groups):
    ring_bits = [("ring", b) for b in range(ring.bit_length() - 1)]
    group_bits = [("fsdp", b) for b in reversed(range(groups.bit_length() - 1))]
    near, far = ring_bits[:1], ring_bits[1:]
    return near + group_bits + far, group_bits + near + far


def norm_scale(values, gain):
    return values * lax.rsqrt(jnp.mean(values * values, axis=-1, keepdims=True) + norm_eps) * gain


def segment_ends(lengths_row, order_row):
    count = lengths_row.shape[0]
    picks = order_row[:, None] == jnp.arange(count, dtype=jnp.int32)[None, :]
    ordered = jnp.sum(jnp.where(picks, lengths_row[None, :], 0), axis=1)
    upto = jnp.arange(count)[:, None] >= jnp.arange(count)[None, :]
    return jnp.sum(jnp.where(upto, ordered[None, :], 0), axis=1)


def segment_of(ends, positions):
    found = jnp.sum((positions[:, None] >= ends[None, :]).astype(jnp.int32), axis=1)
    return jnp.where(positions < 0, -1, found)


def adam_step(weight, first, second, grad, rate, decay):
    momentum = beta_one * first + (1.0 - beta_one) * grad
    variance = beta_two * second + (1.0 - beta_two) * grad * grad
    corrected = momentum / (1.0 - beta_one**STEP)
    scaled = variance / (1.0 - beta_two**STEP)
    return (
        weight - rate * (corrected / (jnp.sqrt(scaled) + adam_eps) + decay * weight),
        momentum,
        variance,
    )


def short_conv(extended, taps, same):
    count = same[0].shape[0]
    result = 0.0
    for shift_by in range(3):
        piece = lax.slice_in_dim(extended, 2 - shift_by, 2 - shift_by + count, axis=0)
        result = result + taps[shift_by][None, :] * piece * same[shift_by]
    return result


def per_device(
    hidden_in, cotangent, mixer_weight, output_weight, updown_weight, down_weight, gain_weight,
    mixer_first, output_first, updown_first, down_first, gain_first,
    mixer_second, output_second, updown_second, down_second, gain_second,
    lengths, seq_order, pad_mask,
):
    ring, groups = lax.axis_size("ring"), lax.axis_size("fsdp")
    ring_id, core = lax.axis_index("ring"), lax.axis_index("core")
    local_rows = hidden_in.shape[1]
    count = 2 * local_rows
    qk_cols = HEADS * FEAT
    half_d, half_qk = D // 2, qk_cols // 2
    d_rows, f_rows = mixer_weight.shape[0], down_weight.shape[0]
    pair_ff = 2 * FF // (2 * ring) // 2
    tables = make_tables()

    def gather(block):
        return lax.all_gather(block, ("ring", "fsdp"), axis=0, tiled=False)

    def to_owner(array):
        blocks = array.reshape(array.shape[:-1] + (ring, 2, groups, d_rows))
        return row_major(blocks.swapaxes(-3, -2).reshape(array.shape))

    def from_owner(array):
        blocks = array.reshape(array.shape[:-1] + (ring, groups, 2, d_rows))
        return row_major(blocks.swapaxes(-3, -2).reshape(array.shape))

    def exchanged(halves):
        return in_order(core, choose(core, *halves), swap(choose(core, *halves[::-1])))

    def column_half(weight, c):
        pieces, at = [], 0
        for width in (qk_cols, qk_cols, D, D, D):
            pieces.append(weight[:, at + c * width // 2 : at + (c + 1) * width // 2])
            at += width
        return jnp.concatenate(pieces, axis=1)

    gain_low = jnp.pad(gain_weight.astype(bf16), ((0, 0), (0, LANES - gain_weight.shape[1])))
    mixer_low = mixer_weight.astype(bf16)
    halves = [jnp.concatenate([column_half(mixer_low, c), gain_low], axis=1) for c in range(2)]
    packed = exchanged(halves).reshape(1, 2 * d_rows, -1)
    updown_low = updown_weight.astype(bf16).reshape(d_rows, 2, ring, 2, pair_ff)
    packed_gate, packed_up = [
        exchanged([updown_low[:, which, :, c].reshape(d_rows, FF // 2) for c in range(2)]) for which in range(2)
    ]
    output_low = to_owner(output_weight.astype(bf16))
    packed_output = exchanged([output_low[:, :half_d], output_low[:, half_d:]])
    gate_w = gather(packed_gate).reshape(D, FF // 2)
    mixer_all, output_w = gather_rows(
        [tie(packed, packed_gate), packed_output],
        [[256, 256] + [512] * 4 + [256, 256], [512, 384]],
        [1],
        ring,
        groups,
    )
    mixer_w, gains = mixer_all[:, : 2 * half_qk + 3 * half_d], mixer_all[:, 2 * half_qk + 3 * half_d :].astype(f32)
    up_w = gather(tie(packed_up, mixer_all)).reshape(D, FF // 2)

    hidden_own, upstream_own = to_owner(hidden_in[0]), to_owner(cotangent[0])
    tokens = in_order(core, hidden_own, swap(hidden_own)).reshape(count, D).astype(f32)
    upstream = in_order(core, upstream_own, swap(upstream_own)).reshape(count, D)

    ends = segment_ends(lengths[0], seq_order[0])
    start = ring_id * count
    segment = segment_of(ends, start + jnp.arange(-2, count, dtype=jnp.int32))
    seg = segment[2:]
    keep = lax.dynamic_slice_in_dim(pad_mask[0], start, count).astype(f32)
    tails = segment_of(ends, jnp.arange(1, ring + 1, dtype=jnp.int32) * count - 1)
    on = (seg == segment[1]).astype(f32)
    fresh = jnp.where(seg == seg[count - 1], keep, 0.0)
    row_ids = lax.broadcasted_iota(jnp.int32, (count, count), 0)
    col_ids = lax.broadcasted_iota(jnp.int32, (count, count), 1)
    allow = jnp.where((seg[:, None] == seg[None, :]) & (col_ids <= row_ids), keep[None, :], 0.0).astype(bf16)
    same = [(segment[2 - s : 2 - s + count] == seg).astype(f32)[:, None] for s in range(3)]
    before = jnp.concatenate([jnp.full((1,), -1, jnp.int32), tails[:-1]])
    chips = jnp.arange(ring)
    link = ((before[:, None] == tails[None, :]) & (chips[None, :] < chips[:, None])).astype(f32)

    def per_head(block):
        wide = block.reshape(count, HALF_HEADS, HEAD_WIDTH).transpose(1, 0, 2)
        return jnp.pad(wide, ((0, 0), (0, 0), (0, LANES - HEAD_WIDTH)))

    def from_heads(block):
        return block[:, :, :HEAD_WIDTH].transpose(1, 0, 2).reshape(count, half_d)

    normed_f, norm1_back = jax.vjp(norm_scale, tokens, gains[:, 0])
    normed = normed_f.astype(bf16)
    proj = jnp.dot(normed, mixer_w, preferred_element_type=f32)
    down_w = gather(tie(to_owner(down_weight.astype(bf16)), proj)).reshape(FF // 2, D)
    query = proj[:, :half_qk].astype(bf16)
    key_vecs = proj[:, half_qk : 2 * half_qk].astype(bf16)
    value = proj[:, 2 * half_qk : 2 * half_qk + half_d].astype(bf16)
    conv_in = proj[:, 2 * half_qk + half_d : 2 * half_qk + 2 * half_d].astype(bf16)
    gate = proj[:, 2 * half_qk + 2 * half_d :]
    key_t = key_vecs.T
    lane = jnp.arange(LANES)
    values = jnp.where(lane == HEAD_WIDTH, jnp.ones((), bf16), per_head(value))
    att, den, carry, halo = attend(
        link, tie(query, gate_w), key_t, values, allow, on[:, None], fresh[None, :], conv_in[count - 16 :],
        tables, ring,
    )
    halo = jnp.where(ring_id == 0, jnp.zeros((), bf16), halo[14:])
    extended = jnp.concatenate([halo, conv_in], axis=0).astype(f32)
    taps = lax.dynamic_slice_in_dim(from_owner(gains[:, 2:5].T), core * half_d, half_d, axis=1)

    def gating(ext_in, taps_in, gate_in):
        return short_conv(ext_in, taps_in, same) * jax.nn.sigmoid(gate_in)

    gated, gate_back = jax.vjp(gating, extended, taps, gate)
    mix_half = (from_heads(att).astype(f32) + gated).astype(bf16)
    mix_other = swap(mix_half)
    output_half = lax.dynamic_slice_in_dim(output_w, core * half_d, half_d, axis=0)
    output_other = lax.dynamic_slice_in_dim(output_w, (1 - core) * half_d, half_d, axis=0)
    branch = dot_nn(mix_half, output_half) + dot_nn(mix_other, output_other)
    middle = tokens + branch
    normed2_f, norm2_back = jax.vjp(norm_scale, middle, gains[:, 1])
    normed2 = normed2_f.astype(bf16)
    gate_in, up_in = dot_nn(normed2, gate_w), dot_nn(normed2, up_w)

    def swiglu(gate_part, up_part):
        return jax.nn.silu(gate_part) * up_part

    inner_f, inner_back = jax.vjp(swiglu, gate_in, up_in)
    inner = inner_f.astype(bf16)
    feed_part = jnp.dot(inner, down_w, preferred_element_type=f32)

    def own_rows(block):
        return lax.dynamic_slice_in_dim(block, core * local_rows, local_rows, axis=0)

    def other_rows(block):
        return lax.dynamic_slice_in_dim(block, (1 - core) * local_rows, local_rows, axis=0)

    def by_owner(grad, rows):
        blocks = grad.reshape(ring, groups, rows, grad.shape[-1])
        return jnp.pad(blocks, ((0, 0), (0, 0), (0, -rows % 16), (0, 0)))

    def inner_dot(left_mat, right_mat):
        return dot_tn(left_mat, right_mat).astype(bf16)

    orders = both_orders(ring, groups)

    def column_parts(left_mat, right_mat, rows):
        cut = right_mat.shape[1] // 2
        return [by_owner(inner_dot(left_mat, part), rows) for part in (right_mat[:, :cut], right_mat[:, cut:])]

    down_chain = Halving(column_parts(inner, upstream, f_rows), orders)
    down_chain.step()
    upstream_after = upstream
    for one in down_chain.step():
        upstream_after = tie(upstream_after, one)
    inner_grad = dot_nt(upstream_after, down_w).astype(bf16)
    gate_part_grad, up_part_grad = [g.astype(bf16) for g in inner_back(inner_grad.astype(f32))]
    updown_parts = [by_owner(inner_dot(normed2, g), 2 * d_rows) for g in (gate_part_grad, up_part_grad)]
    updown_chain = Halving(updown_parts, orders)
    updown_sent = updown_chain.step()
    for one in updown_sent + down_chain.step(updown_sent[1]):
        gate_part_grad = tie(gate_part_grad, one)
    normed2_part = (dot_nt(gate_part_grad, gate_w) + dot_nt(up_part_grad, up_w)).astype(bf16)
    normed2_grad = normed2_part.astype(f32) + swap(normed2_part).astype(f32)
    middle_part, gain2_grad = norm2_back(normed2_grad)
    middle_grad = upstream.astype(f32) + middle_part
    branch_grad = middle_grad.astype(bf16)
    output_part = inner_dot(mix_half, branch_grad).reshape(ring // 2, 2, groups * d_rows, D)
    output_keep = lax.dynamic_index_in_dim(output_part, core, axis=1, keepdims=False)
    output_send = lax.dynamic_index_in_dim(output_part, 1 - core, axis=1, keepdims=False)
    output_part = in_order(core, output_keep, swap(output_send)).reshape(ring, groups, d_rows, D)
    output_part = jnp.concatenate([output_part[..., :half_d], output_part[..., half_d:]], axis=2)
    output_part = by_owner(output_part.reshape(D, half_d), 2 * d_rows)
    mix_grad = dot_nt(branch_grad, output_half).astype(bf16)
    ext_grad, taps_grad, gate_grad = gate_back(mix_grad.astype(f32))
    head_grad = mix_grad
    for one in updown_chain.step():
        head_grad = tie(head_grad, one)
    query_g, key_g, value_g, after = attend_back(
        link, query, key_vecs, query.T, key_t, values, per_head(head_grad), att, den, carry, allow, on[:, None],
        on[None, :], fresh[:, None], ext_grad[:8], tables, ring, [],
    )
    sent = updown_chain.step(key_g) + down_chain.step(key_g)
    after = jnp.where(ring_id == ring - 1, 0.0, after[:2])
    conv_grad = ext_grad[2:] + jnp.pad(after, ((count - 2, 0), (0, 0)))
    proj_grad = jnp.concatenate(
        [
            query_g.astype(bf16), key_g.astype(bf16), from_heads(value_g),
            conv_grad.astype(bf16), gate_grad.astype(bf16),
        ],
        axis=1,
    )
    for one in sent:
        proj_grad = tie(proj_grad, one)
    mixer_part = by_owner(inner_dot(normed, proj_grad), 2 * d_rows)
    normed_part = dot_nt(proj_grad, mixer_w)
    normed_grad = own_rows(normed_part) + swap(other_rows(normed_part))
    tokens_own = own_rows(tokens)
    ignored, norm1_back_own = jax.vjp(norm_scale, tokens_own, gains[:, 0])
    input_part, gain1_grad = norm1_back_own(normed_grad)
    input_grad = from_owner(own_rows(middle_grad) + input_part)

    keys = sorted(updown_chain.place, key=updown_chain.place.get)

    def by_bits(partial):
        return partial.reshape((2,) * len(keys) + partial.shape[2:])

    arrays, specs, widths = [], [], []

    def add_chains(array, columns, chain_keys, chain_orders, ranks):
        at = 0
        for number, width in enumerate(columns):
            specs.append((len(arrays), at, width, chain_keys, chain_orders[number % len(chain_orders)], ranks[number]))
            at += width
        arrays.append(array)
        widths.append(len(columns))

    for number, (left, left_keys, order) in enumerate(updown_chain.rest()):
        add_chains(left, [FF // 4, FF // 4], left_keys, [order], [number / 2, 1 + number / 2])
    add_chains(by_bits(mixer_part), [512] * 5 + [384], keys, orders, [0.0, 0.0, 1.0, 1.0, 2.0, 2.0])
    add_chains(by_bits(output_part), [512, 384], keys, orders, [3.0, 3.0])
    summed = reduce_rest(arrays, specs)
    wholes = []
    for number in widths:
        wholes.append(jnp.concatenate(summed[:number], axis=1))
        summed = summed[number:]
    updown_sum = jnp.concatenate(wholes[:2], axis=1)
    down_sum = from_owner(down_chain.result()[:f_rows])
    mixer_sum = wholes[2]
    output_sum = from_owner(
        wholes[3][: 2 * d_rows].reshape(2, d_rows, half_d).transpose(1, 0, 2).reshape(d_rows, D)
    )

    feed = own_rows(feed_part) + swap(tie(other_rows(feed_part), key_g))
    middle_own = own_rows(middle)
    layer = from_owner((middle_own + feed).astype(bf16))
    branch_own = own_rows(branch)
    stats = jnp.stack([jnp.sum(middle_own * middle_own), jnp.sum(branch_own * branch_own), jnp.sum(feed * feed)])

    taps_wide = lax.dynamic_update_slice(jnp.zeros((3, D), f32), taps_grad, (0, core * half_d))
    gain_grad = jnp.concatenate([from_owner(jnp.stack([gain1_grad, 0.5 * gain2_grad])), taps_wide], axis=0)

    square = functools.reduce(jnp.add, [jnp.sum(g * g) for g in (mixer_sum, updown_sum, down_sum, output_sum)])
    spots = jnp.arange(D)[None, :]
    numbers = functools.reduce(
        jnp.add, [jnp.where(spots == i, n, 0.0) for i, n in enumerate((square, stats[0], stats[1], stats[2]))]
    )
    sums = sum_everywhere(jnp.concatenate([gain_grad, numbers, jnp.zeros((2, D), f32)], axis=0), ring, groups)
    gain_total = sums[:5]
    total_sq = sums[5, 0] + jnp.sum(gain_total * gain_total)
    stat_sum = sums[5, 1:4]
    place = (ring_id * 2 + core) * groups + lax.axis_index("fsdp")
    gain_sum = lax.dynamic_index_in_dim(
        gain_total.reshape(5, 2 * ring * groups, d_rows), place, axis=1, keepdims=False
    ).T

    def own_whole(summed):
        blocks = summed[: 2 * d_rows].reshape(2, d_rows, summed.shape[-1])
        keep_rows = lax.dynamic_index_in_dim(blocks, core, axis=0, keepdims=False)
        send_rows = lax.dynamic_index_in_dim(blocks, 1 - core, axis=0, keepdims=False)
        return in_order(core, keep_rows, swap(send_rows))

    mixer_own = own_whole(mixer_sum)
    pieces, at = [], 0
    for width in (half_qk, half_qk, half_d, half_d, half_d):
        pieces += [mixer_own[0, :, at : at + width], mixer_own[1, :, at : at + width]]
        at += width
    mixer_own = jnp.concatenate(pieces, axis=1)
    updown_own = own_whole(updown_sum).reshape(2, d_rows, 2, ring, pair_ff)
    updown_own = updown_own.transpose(1, 2, 3, 0, 4).reshape(d_rows, 2 * FF)
    grad_list = (mixer_own, output_sum, updown_own, down_sum, gain_sum)
    grad_norm = jnp.sqrt(total_sq)
    factor = jnp.minimum(1.0, clip_level / grad_norm)
    masters = (mixer_weight, output_weight, updown_weight, down_weight, gain_weight)
    firsts = (mixer_first, output_first, updown_first, down_first, gain_first)
    seconds = (mixer_second, output_second, updown_second, down_second, gain_second)
    nexts, moms, varis = ([], [], [])
    for index in range(5):
        rate = rate_gain if index == 4 else rate_matrix
        decay = 0.0 if index == 4 else decay_rate
        new_w, new_m, new_v = adam_step(
            masters[index], firsts[index], seconds[index], grad_list[index] * factor, rate, decay
        )
        nexts.append(new_w)
        moms.append(new_m)
        varis.append(new_v)
    layer_rms = jnp.sqrt(stat_sum / (count * ring * groups * D))
    return (layer[None], input_grad[None], *nexts, *moms, *varis, grad_norm, layer_rms)


def solution(mesh):
    shards, groups = mesh.shape["seq"], mesh.shape["fsdp"]
    split = Mesh(mesh.devices.reshape(shards // 2, 2, groups), ("ring", "core", "fsdp"))
    tokens = P("fsdp", ("ring", "core"), None)
    rows = P(("ring", "core", "fsdp"), None)
    pack = P("fsdp", None)
    return jax.shard_map(
        per_device,
        mesh=split,
        in_specs=(tokens,) * 2 + (rows,) * 15 + (pack,) * 3,
        out_specs=(tokens,) * 2 + (rows,) * 15 + (P(), P()),
        check_vma=False,
    )
```
